256 devices in a mesh: row: 8 (over y, core), col: 32 (over x, z).
Axes of the slice: x: 4, y: 4, z: 8, core: 2. Of those that a mesh axis runs over, the one named last changes fastest.
Arguments:
- stars: float32 [13, 524288], P(None, ('row', 'col')), may hold values from -5 to 5, as said below
- elapsed: float32 [524288], P(('row', 'col')), may hold values from 0.0625 to 0.5
- active_ids: int32 [4096], P('row'), may hold values from 0 to 524287, as said below
Outputs:
- updated_stars: float32 [13, 524288], P(None, ('row', 'col'))
The draws below stay inside these ranges and needn't reach their ends.
Inputs may be any that keep to these rules, and one draw needn't show every extreme that they name: Rows 0 to 11 of stars hold positions, velocities, accelerations and jerks; row 12 holds masses between 0.2 / 524288 and 2 / 524288. `active_ids`: the indices are distinct.
All inputs are finite; a program needn't handle non-finite values.
Results may differ from the reference program's by a relative error of at most 0.0001.
Values sent between devices are 32-bit elements; how exact they have to be, the bound alone decides.
A program may use at most 64 MiB of HBM per device.

```python
import math
import jax
import jax.numpy as jnp
from jax import lax

NSTARS = 524288
ACTIVE = 4096


def draw_stars(key, part):
    key = jax.random.fold_in(key, 11)
    first, second = jax.random.split(key)
    motion = jnp.clip(jax.random.normal(first, (12, NSTARS), jnp.float32), -5.0, 5.0)
    masses = jnp.exp(jax.random.uniform(second, (1, NSTARS), jnp.float32, math.log(0.2), math.log(2.0))) / NSTARS
    return jnp.concatenate([motion, masses], 0)


def draw_active_ids(key, part):
    key = jax.random.fold_in(key, 23)
    first, second = jax.random.split(key)
    inner = 1 + jax.random.permutation(first, NSTARS - 2)[:ACTIVE - 2]
    chosen = jnp.concatenate([jnp.array([0, NSTARS - 1], jnp.int32), inner.astype(jnp.int32)])
    return jax.random.permutation(second, chosen).astype(jnp.int32)


def shard_levels(rng, shape, cuts, smallest, top_value):
    level, own = 1.0, jax.random.fold_in(rng, 6)
    for axis_at, shards_of in cuts:
        heights = jnp.exp(jax.random.uniform(jax.random.fold_in(own, axis_at), (shards_of,), jnp.float32, smallest / len(cuts), top_value / len(cuts)))
        level = level * jnp.repeat(heights, shape[axis_at] // shards_of).reshape([-1 if axis == axis_at else 1 for axis in range(len(shape))])
    return level


def setup_inputs(seed: int = 0) -> dict:
    splits = jax.random.split(jax.random.key(seed), 4)
    return {
        "stars": draw_stars(jax.random.fold_in(splits[3], 71), 0),
        "elapsed": jnp.clip(0.0625 + 0.4375 * jax.random.uniform(splits[1], (NSTARS,), jnp.float32) ** shard_levels(splits[1], (NSTARS,), ((0, 256),), -0.2, 0.2), 0.0625, 0.5),
        "active_ids": draw_active_ids(jax.random.fold_in(splits[3], 71), 0),
    }


SOFTEN = 0.0025

def predict(position, velocity, accel_old, jerk_old, elapsed):
    pos_pred = position + elapsed * (velocity + elapsed * (accel_old / 2.0 + elapsed * jerk_old / 6.0))
    vel_pred = velocity + elapsed * (accel_old + elapsed * jerk_old / 2.0)
    return (pos_pred, vel_pred)

def pair_terms(act_pos, act_vel, fld_pos, fld_vel, fld_mass):
    offset = fld_pos[:, None, :] - act_pos[:, :, None]
    relvel = fld_vel[:, None, :] - act_vel[:, :, None]
    dist_sq = lax.optimization_barrier(jnp.sum(offset * offset, 0)) + SOFTEN
    inverse = lax.rsqrt(dist_sq)
    weight = fld_mass[None, :] * inverse * inverse * inverse
    radial = 3.0 * lax.optimization_barrier(jnp.sum(offset * relvel, 0)) * inverse * inverse
    accels = lax.optimization_barrier(jnp.sum(weight[None] * offset, -1))
    jerk_sum = lax.optimization_barrier(jnp.sum(weight[None] * (relvel - radial[None] * offset), -1))
    return jnp.concatenate([accels, jerk_sum], 0)

def corrector(pos_old, vel_old, acc_old, jerk_old, step_len, acc_new, jerk_new):
    vel_new = vel_old + (acc_old + acc_new) * step_len / 2.0 + (jerk_old - jerk_new) * step_len * step_len / 12.0
    pos_new = pos_old + (vel_old + vel_new) * step_len / 2.0 + (acc_old - acc_new) * step_len * step_len / 12.0
    return jnp.concatenate([pos_new, vel_new, acc_new, jerk_new], 0)

def reference(stars, elapsed, active_ids):
    pos_pred, vel_pred = predict(stars[0:3], stars[3:6], stars[6:9], stars[9:12], elapsed[None, :])
    masses = stars[12]
    picked = jnp.take(stars, active_ids, axis=1)
    step_len = jnp.take(elapsed, active_ids)[None, :]
    act_pos, act_vel = predict(picked[0:3], picked[3:6], picked[6:9], picked[9:12], step_len)
    block_len = math.gcd(NSTARS, 16384)
    nblocks = NSTARS // block_len
    field_pos = pos_pred.reshape(3, nblocks, block_len).transpose(1, 0, 2)
    field_vel = vel_pred.reshape(3, nblocks, block_len).transpose(1, 0, 2)
    field_mass = masses.reshape(nblocks, block_len)
    tile_len = math.gcd(ACTIVE, 128)
    ntiles = ACTIVE // tile_len
    tiles_pos = act_pos.reshape(3, ntiles, tile_len).transpose(1, 0, 2)
    tiles_vel = act_vel.reshape(3, ntiles, tile_len).transpose(1, 0, 2)

    def one_tile(tile_pair):
        tile_pos, tile_vel = tile_pair

        def add_block(running, field_block):
            block_pos, block_vel, block_mass = field_block
            return (running + pair_terms(tile_pos, tile_vel, block_pos, block_vel, block_mass), None)
        running, _ = lax.scan(add_block, jnp.zeros((6, tile_len), jnp.float32), (field_pos, field_vel, field_mass))
        return running
    totals = lax.map(one_tile, (tiles_pos, tiles_vel))
    totals = totals.transpose(1, 0, 2).reshape(6, ACTIVE)
    corrected = corrector(picked[0:3], picked[3:6], picked[6:9], picked[9:12], step_len, totals[0:3], totals[3:6])
    return stars.at[0:12, active_ids].set(corrected)
```

```python
import functools

import jax
import jax.numpy as jnp
from jax import lax
from jax.experimental import pallas as pl
from jax.experimental.pallas import tpu as pltpu
from jax.sharding import PartitionSpec as P

SOFTEN = 0.0025
F32 = jnp.float32
BF16 = jnp.bfloat16
ROWS = 8
XS = 4
ZS = 8
STARS = 2048
ACT = 512
CHUNK = 256
SPLIT_PAIRS = ((0, 0), (0, 1), (1, 0), (1, 1), (0, 2), (2, 0))
VMEM = pl.BlockSpec(memory_space=pltpu.VMEM)


def split3(x):
    hi = x.astype(BF16).astype(F32)
    rest = x - hi
    mid = rest.astype(BF16).astype(F32)
    return hi, mid, rest - mid


def place():
    row = lax.axis_index("row")
    col = lax.axis_index("col")
    return row, col, col // ZS, col % ZS


def row_peer(o):
    row, col, _, _ = place()
    return (lax.rem(row + o, ROWS), col)


def x_peer(o):
    row, _, x, z = place()
    return (row, lax.rem(x + o, XS) * ZS + z)


def z_peer(o):
    row, _, x, z = place()
    return (row, x * ZS + lax.rem(z + o, ZS))


def enter():
    barrier = pltpu.get_barrier_semaphore()
    peers = (
        [row_peer(o) for o in range(1, ROWS)]
        + [x_peer(o) for o in range(1, XS)]
        + [z_peer(o) for o in range(1, ZS)]
    )
    for peer in peers:
        pl.semaphore_signal(barrier, inc=1, device_id=peer, device_id_type=pl.DeviceIdType.MESH)
    pl.semaphore_wait(barrier, len(peers))


def send(src, dst, send_sem, recv_sem, peer):
    copy = pltpu.make_async_remote_copy(
        src_ref=src,
        dst_ref=dst,
        send_sem=send_sem,
        recv_sem=recv_sem,
        device_id=peer,
        device_id_type=pl.DeviceIdType.MESH,
    )
    copy.start()
    return copy


def sum_over_col(own, x_in, mid, z_in, xs, xr, zs, zr):
    copies = [
        send(own, x_in.at[o - 1], xs.at[o - 1], xr.at[o - 1], x_peer(o)) for o in range(1, XS)
    ]
    for c in copies:
        c.wait()
    mid[...] = (own[...] + x_in[0]) + (x_in[1] + x_in[2])
    copies = [
        send(mid, z_in.at[o - 1], zs.at[o - 1], zr.at[o - 1], z_peer(o)) for o in range(1, ZS)
    ]
    for c in copies:
        c.wait()
    return ((mid[...] + z_in[0]) + (z_in[1] + z_in[2])) + (
        (z_in[3] + z_in[4]) + (z_in[5] + z_in[6])
    )


def gather_kernel(
    stars, elapsed, ids, field, act, own, x_in, mid, z_in, rs, rr, xs, xr, zs, zr
):
    row, col, _, _ = place()
    t = elapsed[...]
    enter()
    x, v, a, j = stars[0:3, :], stars[3:6, :], stars[6:9, :], stars[9:12, :]
    field[row, 0:3, :] = x + t * (v + t * (a / 2.0 + t * j / 6.0))
    field[row, 3:6, :] = v + t * (a + t * j / 2.0)
    field[row, 6:7, :] = stars[12:13, :]
    field[row, 7:8, :] = jnp.zeros((1, STARS), F32)
    copies = [
        send(field.at[row], field.at[row], rs.at[o - 1], rr.at[o - 1], row_peer(o))
        for o in range(1, ROWS)
    ]
    star = ids[...]
    owner = star // STARS
    group = star % STARS // 128
    lane = star % 128
    here = owner % 32 == col
    code = jnp.where(here, owner // 32 * 16 + group, -1)
    one_hot = jnp.where(
        lax.broadcasted_iota(jnp.int32, (128, ACT), 0) == lane, 1.0, 0.0
    ).astype(BF16)
    one_hot = jnp.concatenate([one_hot] * 3, 0)
    for c in copies:
        c.wait()

    def pick(r, total):
        block = jnp.concatenate([field[r, :, g * 128 : (g + 1) * 128] for g in range(16)], 0)
        parts = jnp.concatenate(split3(block), 1).astype(BF16)
        found = jnp.dot(parts, one_hot, preferred_element_type=F32)
        for g in range(16):
            total = total + jnp.where(code == r * 16 + g, found[g * 8 : (g + 1) * 8], 0.0)
        return total

    own[...] = lax.fori_loop(0, ROWS, pick, jnp.zeros((8, ACT), F32))
    act[...] = sum_over_col(own, x_in, mid, z_in, xs, xr, zs, zr)


def dither(lanes):
    return 1.0 + ((lanes * 40503) & 65535).astype(F32) * (1.0 / 65536.0)


def pair_kernel(field, act, out, bmat, rmat, acol, xib, accum, d0, d1, w0, w1):
    total = field[0]
    for r in range(1, ROWS):
        total = total + field[r]
    centre = jnp.sum(total, axis=1, keepdims=True) / (ROWS * STARS)
    cx, cv = centre[0:3], centre[3:6]
    xa, va = act[0:3, :] - cx, act[3:6, :] - cv
    sa = jnp.sum(xa * va, axis=0, keepdims=True)
    parts = split3(jnp.concatenate([-xa, -va, jnp.ones_like(sa), sa], 0))
    stacked = jnp.concatenate([parts[p] for p, _ in SPLIT_PAIRS] + [jnp.zeros((80, ACT), F32)], 0)
    acol[...] = jnp.transpose(stacked).astype(BF16)
    turned = jnp.transpose(jnp.concatenate([act[...], jnp.zeros((120, ACT), F32)], 0))
    for k in range(3):
        xib[k] = jnp.broadcast_to(turned[:, k : k + 1], (ACT, 128))
    lanes = lax.broadcasted_iota(jnp.int32, (1, STARS), 1)
    per_slot = STARS // CHUNK

    def operands(r, _):
        f = field[r]
        xf, vf, mass = f[0:3] - cx, f[3:6] - cv, f[6:7]
        sf = jnp.sum(xf * vf, axis=0, keepdims=True)
        b = split3(jnp.concatenate([vf, xf, sf, jnp.ones_like(sf)], 0))
        b = jnp.concatenate([b[q] for _, q in SPLIT_PAIRS] + [jnp.zeros((80, STARS), F32)], 0)
        b = b.astype(BF16)
        m = mass / dither(lanes)
        zero = jnp.zeros_like(m)
        by_w = jnp.concatenate([m * xf, m * vf, m, zero], 0)
        by_v = jnp.concatenate([zero, zero, zero, -3.0 * m * xf, zero, -3.0 * m], 0)
        pad = jnp.zeros((8, STARS), F32)
        by_w = jnp.concatenate(list(split3(by_w)) + [pad], 0).astype(BF16)
        by_v = jnp.concatenate(list(split3(by_v)) + [pad], 0).astype(BF16)
        for c in range(per_slot):
            cut = slice(c * CHUNK, (c + 1) * CHUNK)
            bmat[r * per_slot + c] = b[:, cut]
            rmat[r * per_slot + c] = jnp.concatenate([by_w[:, cut], by_v[:, cut]], 1)
        return 0

    lax.fori_loop(0, ROWS, operands, 0)
    accum[...] = jnp.zeros_like(accum)
    w1[...] = jnp.zeros_like(w1)
    lane = lax.broadcasted_iota(jnp.int32, (1, CHUNK), 1)
    chunks = ROWS * per_slot

    def radial(c, dst):
        dst[...] = jnp.dot(acol[...], bmat[c], preferred_element_type=F32)

    def sums(c, src):
        accum[...] += lax.dot_general(
            src[...], rmat[c], (((1,), (1,)), ((), ())), preferred_element_type=F32
        )

    def step(c, d_next, d_now, w_now, w_before):
        r = c // per_slot
        off = pl.multiple_of(c % per_slot * CHUNK, CHUNK)
        factor = dither(lane + off)
        xs = [field[r, pl.ds(k, 1), pl.ds(off, CHUNK)] for k in range(3)]
        radial(jnp.minimum(c + 1, chunks - 1), d_next)
        for h in range(CHUNK // 128):
            cut = slice(h * 128, (h + 1) * 128)
            dx, dy, dz = [xs[k][:, cut] - xib[k] for k in range(3)]
            q = (dx * dx + SOFTEN) + dy * dy + dz * dz
            inv = lax.rsqrt(q)
            inv2 = inv * inv
            w = (inv * factor[:, cut]) * inv2
            w_now[:, cut] = w.astype(BF16)
            w_now[:, CHUNK + h * 128 : CHUNK + (h + 1) * 128] = (
                w * (inv2 * d_now[:, cut])
            ).astype(BF16)
        sums(jnp.maximum(c - 1, 0), w_before)

    radial(0, d0)

    def two(i, _):
        step(2 * i, d1, d0, w0, w1)
        step(2 * i + 1, d0, d1, w1, w0)
        return 0

    lax.fori_loop(0, chunks // 2, two, 0)
    sums(chunks - 1, w1)
    o = jnp.transpose(jnp.concatenate([accum[...], jnp.zeros((ACT, 96), F32)], 1))
    o = o[0:8] + o[8:16] + o[16:24]
    out[0:3, :] = o[0:3] - xa * o[6:7]
    out[3:6, :] = o[3:6] - va * o[6:7] - xa * o[7:8]
    out[6:8, :] = jnp.zeros((2, ACT), F32)


def finish_kernel(
    part, ids, stars, elapsed, out, tot, x_in, mid, z_in, rs, rr, xs, xr, zs, zr
):
    row, col, _, _ = place()
    enter()
    total = sum_over_col(part, x_in, mid, z_in, xs, xr, zs, zr)
    tot[row, 0:6, :] = total[0:6]
    tot[row, 6:7, :] = ids[...].astype(F32)
    tot[row, 7:8, :] = jnp.ones((1, ACT), F32)
    copies = [
        send(tot.at[row], tot.at[row], rs.at[o - 1], rr.at[o - 1], row_peer(o))
        for o in range(1, ROWS)
    ]
    for c in copies:
        c.wait()
    first = (row * 32 + col) * STARS
    sub = lax.broadcasted_iota(jnp.int32, (128, ACT), 0)

    def scatter(r, sums):
        local = tot[r, 6:7, :].astype(jnp.int32) - first
        owned = (local >= 0) & (local < STARS)
        group = jnp.where(owned, local // 128, -1)
        one_hot = jnp.where(sub == local % 128, 1.0, 0.0).astype(BF16)
        parts = jnp.concatenate(split3(tot[r]), 0)
        lhs = jnp.concatenate(
            [jnp.where(group == g, parts, 0.0).astype(BF16) for g in range(16)], 0
        )
        return sums + lax.dot_general(
            lhs, one_hot, (((1,), (1,)), ((), ())), preferred_element_type=F32
        )

    placed = lax.fori_loop(0, ROWS, scatter, jnp.zeros((384, 128), F32))
    new = jnp.concatenate(
        [
            placed[g * 24 : g * 24 + 8]
            + placed[g * 24 + 8 : g * 24 + 16]
            + placed[g * 24 + 16 : g * 24 + 24]
            for g in range(16)
        ],
        1,
    )
    acc_new, jerk_new, hit = new[0:3], new[3:6], new[7:8] > 0.5
    t = elapsed[...]
    x, v, a, j = stars[0:3, :], stars[3:6, :], stars[6:9, :], stars[9:12, :]
    v1 = v + (a + acc_new) * t / 2.0 + (j - jerk_new) * t * t / 12.0
    x1 = x + (v + v1) * t / 2.0 + (a - acc_new) * t * t / 12.0
    out[0:3, :] = jnp.where(hit, x1, x)
    out[3:6, :] = jnp.where(hit, v1, v)
    out[6:9, :] = jnp.where(hit, acc_new, a)
    out[9:12, :] = jnp.where(hit, jerk_new, j)
    out[12:13, :] = stars[12:13, :]


def exchange_scratch():
    dma = pltpu.SemaphoreType.DMA
    return [
        pltpu.VMEM((XS - 1, 8, ACT), F32),
        pltpu.VMEM((8, ACT), F32),
        pltpu.VMEM((ZS - 1, 8, ACT), F32),
        dma((ROWS - 1,)),
        dma((ROWS - 1,)),
        dma((XS - 1,)),
        dma((XS - 1,)),
        dma((ZS - 1,)),
        dma((ZS - 1,)),
    ]


def local(stars, elapsed, active_ids):
    elapsed = elapsed.reshape(1, STARS)
    ids = active_ids.reshape(1, ACT)
    field, act = pl.pallas_call(
        gather_kernel,
        out_shape=(
            jax.ShapeDtypeStruct((ROWS, 8, STARS), F32),
            jax.ShapeDtypeStruct((8, ACT), F32),
        ),
        in_specs=[VMEM] * 3,
        out_specs=(VMEM, VMEM),
        scratch_shapes=[pltpu.VMEM((8, ACT), F32)] + exchange_scratch(),
        compiler_params=pltpu.CompilerParams(
            collective_id=0, has_side_effects=True, vmem_limit_bytes=32 << 20
        ),
        name="gather_active",
    )(stars, elapsed, ids)
    part = pl.pallas_call(
        pair_kernel,
        out_shape=jax.ShapeDtypeStruct((8, ACT), F32),
        in_specs=[VMEM] * 2,
        out_specs=VMEM,
        scratch_shapes=[
            pltpu.VMEM((64, 128, CHUNK), BF16),
            pltpu.VMEM((64, 32, 2 * CHUNK), BF16),
            pltpu.VMEM((ACT, 128), BF16),
            pltpu.VMEM((3, ACT, 128), F32),
            pltpu.VMEM((ACT, 32), F32),
            pltpu.VMEM((ACT, CHUNK), F32),
            pltpu.VMEM((ACT, CHUNK), F32),
            pltpu.VMEM((ACT, 2 * CHUNK), BF16),
            pltpu.VMEM((ACT, 2 * CHUNK), BF16),
        ],
        compiler_params=pltpu.CompilerParams(vmem_limit_bytes=40 << 20),
        name="pair_sums",
    )(field, act)
    return pl.pallas_call(
        finish_kernel,
        out_shape=jax.ShapeDtypeStruct((13, STARS), F32),
        in_specs=[VMEM] * 4,
        out_specs=VMEM,
        scratch_shapes=[pltpu.VMEM((ROWS, 8, ACT), F32)] + exchange_scratch(),
        compiler_params=pltpu.CompilerParams(
            collective_id=1, has_side_effects=True, vmem_limit_bytes=32 << 20
        ),
        name="finish_active",
    )(part, ids, stars, elapsed)


def solution(mesh):
    in_specs = (P(None, ("row", "col")), P(("row", "col")), P("row"))
    out_specs = P(None, ("row", "col"))
    return jax.shard_map(local, mesh=mesh, in_specs=in_specs, out_specs=out_specs, check_vma=False)
```

```python
import jax
import jax.numpy as jnp
import numpy as np
from jax import lax
from jax.experimental import pallas as pl
from jax.experimental.pallas import tpu as pltpu
from jax.sharding import PartitionSpec as P

SOFTEN = 0.0025
F32 = jnp.float32
BF16 = jnp.bfloat16
ROWS = 8
YS = 4
XS = 4
ZS = 8
COLS = XS * ZS
STARS = 2048
ACT = 512
CHUNK = 256
PER_SLOT = STARS // CHUNK
CHUNKS = ROWS * PER_SLOT
UNROLL = 4
BLOCK = 64
SPAN = 256
GROUPS = STARS // SPAN
SPLIT_PAIRS = ((0, 0), (0, 1), (1, 0), (1, 1), (0, 2), (2, 0))
SOFTEN_HI = float(np.float32(SOFTEN).astype(jnp.bfloat16))
SOFTEN_LO = float(np.float32(SOFTEN - SOFTEN_HI).astype(jnp.bfloat16))
VMEM = pl.BlockSpec(memory_space=pltpu.VMEM)
HBM = pl.BlockSpec(memory_space=pl.ANY)


def split3(x):
    hi = x.astype(BF16).astype(F32)
    rest = x - hi
    mid = rest.astype(BF16).astype(F32)
    return hi, mid, rest - mid


def split_grid(x):
    coarse = jnp.floor(x * 8.0 + 0.5) * 0.125
    return coarse, x - coarse


def dot3(a, b):
    return jnp.sum(a * b, axis=0, keepdims=True)


def place():
    row = lax.axis_index("row")
    col = lax.axis_index("col")
    return row, col, row // 2, row % 2, col // ZS, col % ZS


def row_from(o):
    _, _, y, core, _, _ = place()
    return lax.rem(y + YS - o, YS) * 2 + core


def y_peer(o):
    _, col, y, core, _, _ = place()
    return (lax.rem(y + o, YS) * 2 + core, col)


def sibling():
    _, col, y, core, _, _ = place()
    return (y * 2 + 1 - core, col)


def x_peer(o):
    row, _, _, _, x, z = place()
    return (row, lax.rem(x + o, XS) * ZS + z)


def z_peer(o):
    row, _, _, _, x, z = place()
    return (row, x * ZS + lax.rem(z + o, ZS))


def send(src, dst, send_sem, recv_sem, peer):
    copy = pltpu.make_async_remote_copy(
        src_ref=src,
        dst_ref=dst,
        send_sem=send_sem,
        recv_sem=recv_sem,
        device_id=peer,
        device_id_type=pl.DeviceIdType.MESH,
    )
    copy.start()
    return copy


def dither(lanes):
    return 1.0 + ((lanes * 40503) & 127).astype(F32) * (1.0 / 128.0)


def field_rows(x, v):
    coarse, fine = split_grid(x)
    one = jnp.ones_like(x[0:1])
    zero = jnp.zeros_like(one)
    big = split3(dot3(coarse, coarse))
    small = split3(dot3(2.0 * coarse + fine, fine))
    hi, mid, lo = split3(fine)
    radial = split3(jnp.concatenate([v, x, dot3(x, v), one], 0))
    return jnp.concatenate(
        [*big, one, one, one, -2.0 * coarse]
        + [zero] * 7
        + [-2.0 * coarse] * 3
        + [hi, mid, lo, -2.0 * hi, -2.0 * hi, -2.0 * mid, -2.0 * mid, *small]
        + [one] * 5
        + [zero] * 10
        + [radial[q] for _, q in SPLIT_PAIRS]
        + [zero] * 16,
        0,
    )


def active_rows(x, v):
    coarse, fine = split_grid(x)
    one = jnp.ones_like(x[0:1])
    zero = jnp.zeros_like(one)
    big = split3(dot3(coarse, coarse))
    small = split3(dot3(2.0 * coarse + fine, fine))
    hi, mid, lo = split3(fine)
    radial = split3(jnp.concatenate([-x, -v, one, dot3(x, v)], 0))
    for_q = jnp.concatenate(
        [one, one, one, *big, coarse]
        + [zero] * 7
        + [hi, mid, lo]
        + [-2.0 * coarse] * 3
        + [hi, mid, hi, mid, one, one, one, *small, SOFTEN_HI * one, SOFTEN_LO * one]
        + [zero] * 74,
        0,
    )
    for_d = jnp.concatenate(
        [zero] * 64 + [radial[p] for p, _ in SPLIT_PAIRS] + [zero] * 16, 0
    )
    return jnp.concatenate([for_q, for_d], 1).astype(BF16)


def kernel(
    stars_in,
    elapsed_in,
    ids_in,
    out,
    stars,
    elapsed,
    ids,
    field,
    found,
    act_x,
    act_mid,
    act_z,
    feats,
    mix,
    spots,
    act_w,
    factor,
    accum,
    qd0,
    qd1,
    w0,
    w1,
    part,
    sum_x,
    sum_mid,
    sum_z,
    tot,
    in_sem,
    fy_s,
    fy_r,
    fc_s,
    fc_r,
    ax_s,
    ax_r,
    az_s,
    az_r,
    sx_s,
    sx_r,
    sz_s,
    sz_r,
    ty_s,
    ty_r,
    tc_s,
    tc_r,
):
    row, col, _, core, _, _ = place()
    loads = [
        pltpu.make_async_copy(src, dst, in_sem.at[i])
        for i, (src, dst) in enumerate(((stars_in, stars), (elapsed_in, elapsed), (ids_in, ids)))
    ]
    for c in loads:
        c.start()
    barrier = pltpu.get_barrier_semaphore()
    peers = (
        [sibling()]
        + [y_peer(o) for o in range(1, YS)]
        + [x_peer(o) for o in range(1, XS)]
        + [z_peer(o) for o in range(1, ZS)]
    )
    for peer in peers:
        pl.semaphore_signal(barrier, inc=1, device_id=peer, device_id_type=pl.DeviceIdType.MESH)
    for c in loads:
        c.wait()

    t = elapsed[...]
    x, v, a, j = stars[0:3, :], stars[3:6, :], stars[6:9, :], stars[9:12, :]
    x = x + t * (v + t * (a / 2.0 + t * j / 6.0))
    v = v + t * (a + t * j / 2.0)
    field[row, 0:3, :] = x
    field[row, 3:6, :] = v
    field[row, 6:7, :] = stars[12:13, :]
    star = ids[...]
    field[row, 7:8, :] = jnp.concatenate([star.astype(F32), jnp.zeros((1, STARS - ACT), F32)], 1)
    centre_x = jnp.floor(jnp.sum(x, axis=1, keepdims=True) * (8.0 / STARS) + 0.5) * 0.125
    centre_v = jnp.floor(jnp.sum(v, axis=1, keepdims=True) * (8.0 / STARS) + 0.5) * 0.125
    pl.semaphore_wait(barrier, len(peers))

    waits = []
    own = field.at[row]
    over_y = {o: send(own, own, fy_s.at[o - 1], fy_r.at[o - 1], y_peer(o)) for o in (1, 3, 2)}
    over_core = [send(own, own, fc_s.at[0], fc_r.at[0], sibling())]

    owner = star // STARS
    code = jnp.where(owner % COLS == col, owner // COLS * 16 + star % STARS // 128, -1)
    one_hot = jnp.where(
        lax.broadcasted_iota(jnp.int32, (128, ACT), 0) == star % 128, 1.0, 0.0
    ).astype(BF16)
    one_hot = jnp.concatenate([one_hot] * 3, 0)

    def pick(r):
        block = jnp.concatenate([field[r, :, g * 128 : (g + 1) * 128] for g in range(16)], 0)
        parts = jnp.concatenate(split3(block), 1).astype(BF16)
        hits = jnp.dot(parts, one_hot, preferred_element_type=F32)
        total = jnp.zeros((8, ACT), F32)
        for g in range(16):
            total = total + jnp.where(code == r * 16 + g, hits[g * 8 : (g + 1) * 8], 0.0)
        found[...] += total

    found[...] = jnp.zeros_like(found)
    pick(row)
    for o in (1, 3, 2):
        over_y[o].wait_recv()
        block = field.at[row_from(o)]
        over_core.append(send(block, block, fc_s.at[o], fc_r.at[o], sibling()))
        pick(row_from(o))
    for c, o in zip(over_core, (0, 1, 3, 2)):
        c.wait_recv()
        pick(row_from(o) + 1 - 2 * core)
    waits += list(over_y.values()) + over_core

    lanes = lax.broadcasted_iota(jnp.int32, (1, STARS), 1)
    lane_of = lax.broadcasted_iota(jnp.int32, (SPAN, ACT), 0)

    def operands(r, _):
        f = field[r]
        x, v, mass = f[0:3] - centre_x, f[3:6] - centre_v, f[6:7]
        rows = field_rows(x, v)
        for b in range(STARS // 128):
            at = pl.ds(pl.multiple_of(r * STARS + b * 128, 128), 128)
            feats[at, :] = jnp.transpose(rows[:, b * 128 : (b + 1) * 128]).astype(BF16)
        m = mass / dither(lanes & 127)
        zero = jnp.zeros_like(m)
        by_w = jnp.concatenate([m * x, m * v, m, zero], 0)
        m = -3.0 * m
        by_v = jnp.concatenate([zero, zero, zero, m * x, zero, m], 0)
        pad = jnp.zeros((8, STARS), F32)
        by_w = jnp.concatenate([*split3(by_w), pad], 0).astype(BF16)
        by_v = jnp.concatenate([*split3(by_v), pad], 0).astype(BF16)
        for c in range(PER_SLOT):
            cut = slice(c * CHUNK, (c + 1) * CHUNK)
            mix[r * PER_SLOT + c] = jnp.concatenate([by_w[:, cut], by_v[:, cut]], 1)
        at = f[7:8, 0:ACT].astype(jnp.int32) % SPAN
        spots[r] = jnp.where(lane_of == at, 1.0, 0.0).astype(BF16)
        return 0

    copies = [
        send(found, act_x.at[o - 1], ax_s.at[o - 1], ax_r.at[o - 1], x_peer(o))
        for o in range(1, XS)
    ]
    factor[...] = dither(lax.broadcasted_iota(jnp.int32, (128, 128), 0))
    lax.fori_loop(0, 4, operands, 0)
    for c in copies:
        c.wait_recv()
    waits += copies
    act_mid[...] = (found[...] + act_x[0]) + (act_x[1] + act_x[2])
    copies = [
        send(act_mid, act_z.at[o - 1], az_s.at[o - 1], az_r.at[o - 1], z_peer(o))
        for o in range(1, ZS)
    ]
    lax.fori_loop(4, ROWS, operands, 0)
    accum[...] = jnp.zeros_like(accum)
    w1[...] = jnp.zeros_like(w1)
    for c in copies:
        c.wait_recv()
    waits += copies
    act = act_mid[...]
    for o in range(ZS - 1):
        act = act + act_z[o]
    xa, va = act[0:3] - centre_x, act[3:6] - centre_v
    act_w[...] = active_rows(xa, va)

    def sums(c, w):
        accum[...] += jnp.dot(mix[c], w[...], preferred_element_type=F32)

    def step(c, qd, w_now, w_before):
        at = pl.ds(pl.multiple_of(c * CHUNK, CHUNK), CHUNK)
        qd[...] = jnp.dot(feats[at, :], act_w[...], preferred_element_type=F32)
        sums(jnp.maximum(c - 1, 0), w_before)
        for b in range(CHUNK // BLOCK):
            down = slice(b * BLOCK, (b + 1) * BLOCK)
            below = slice(CHUNK + b * BLOCK, CHUNK + (b + 1) * BLOCK)
            f = factor[b * BLOCK % 128 : b * BLOCK % 128 + BLOCK, :]
            for h in range(ACT // 128):
                cut = slice(h * 128, (h + 1) * 128)
                inv = lax.rsqrt(qd[down, cut])
                inv2 = inv * inv
                w = (inv * f) * inv2
                w_now[down, cut] = w.astype(BF16)
                d = qd[down, ACT + h * 128 : ACT + (h + 1) * 128]
                w_now[below, cut] = (w * (inv2 * d)).astype(BF16)

    def steps(i, _):
        for u in range(0, UNROLL, 2):
            step(UNROLL * i + u, qd0, w0, w1)
            step(UNROLL * i + u + 1, qd1, w1, w0)
        return 0

    lax.fori_loop(0, CHUNKS // UNROLL, steps, 0)
    sums(CHUNKS - 1, w1)
    o = accum[...]
    o = o[0:8] + o[8:16] + o[16:24]
    part[0:3, :] = o[0:3] - xa * o[6:7]
    part[3:6, :] = o[3:6] - va * o[6:7] - xa * o[7:8]
    part[6:8, :] = jnp.zeros((2, ACT), F32)

    copies = [
        send(part, sum_x.at[o - 1], sx_s.at[o - 1], sx_r.at[o - 1], x_peer(o))
        for o in range(1, XS)
    ]
    for c in copies:
        c.wait_recv()
    waits += copies
    sum_mid[...] = (part[...] + sum_x[0]) + (sum_x[1] + sum_x[2])
    copies = [
        send(sum_mid, sum_z.at[o - 1], sz_s.at[o - 1], sz_r.at[o - 1], z_peer(o))
        for o in range(1, ZS)
    ]
    for c in copies:
        c.wait_recv()
    waits += copies
    total = ((sum_mid[...] + sum_z[0]) + (sum_z[1] + sum_z[2])) + (
        (sum_z[3] + sum_z[4]) + (sum_z[5] + sum_z[6])
    )
    tot[row, 0:6, :] = total[0:6]
    tot[row, 6:7, :] = jnp.zeros((1, ACT), F32)
    tot[row, 7:8, :] = jnp.ones((1, ACT), F32)
    own = tot.at[row]
    over_y = {o: send(own, own, ty_s.at[o - 1], ty_r.at[o - 1], y_peer(o)) for o in (1, 3, 2)}
    over_core = [send(own, own, tc_s.at[0], tc_r.at[0], sibling())]

    first = (row * COLS + col) * STARS

    def scatter(r):
        local = field[r, 7:8, 0:ACT].astype(jnp.int32) - first
        group = jnp.where((local >= 0) & (local < STARS), local // SPAN, -1)
        parts = jnp.concatenate(split3(tot[r]), 0)
        lhs = jnp.concatenate([jnp.where(group == g, parts, 0.0) for g in range(GROUPS)], 0)
        return lax.dot_general(
            lhs.astype(BF16), spots[r], (((1,), (1,)), ((), ())), preferred_element_type=F32
        )

    placed = scatter(row)
    for o in (1, 3, 2):
        over_y[o].wait_recv()
        block = tot.at[row_from(o)]
        over_core.append(send(block, block, tc_s.at[o], tc_r.at[o], sibling()))
        placed = placed + scatter(row_from(o))
    for c, o in zip(over_core, (0, 1, 3, 2)):
        c.wait_recv()
        placed = placed + scatter(row_from(o) + 1 - 2 * core)
    waits += list(over_y.values()) + over_core
    new = jnp.concatenate(
        [
            placed[g * 24 : g * 24 + 8]
            + placed[g * 24 + 8 : g * 24 + 16]
            + placed[g * 24 + 16 : g * 24 + 24]
            for g in range(GROUPS)
        ],
        1,
    )
    acc_new, jerk_new, hit = new[0:3], new[3:6], new[7:8] > 0.5
    t = elapsed[...]
    x, v, a, j = stars[0:3, :], stars[3:6, :], stars[6:9, :], stars[9:12, :]
    v1 = v + (a + acc_new) * t / 2.0 + (j - jerk_new) * t * t / 12.0
    x1 = x + (v + v1) * t / 2.0 + (a - acc_new) * t * t / 12.0
    out[0:3, :] = jnp.where(hit, x1, x)
    out[3:6, :] = jnp.where(hit, v1, v)
    out[6:9, :] = jnp.where(hit, acc_new, a)
    out[9:12, :] = jnp.where(hit, jerk_new, j)
    out[12:13, :] = stars[12:13, :]
    for c in waits:
        c.wait_send()


def scratch():
    dma = pltpu.SemaphoreType.DMA

    def sums():
        return [
            pltpu.VMEM((8, ACT), F32),
            pltpu.VMEM((XS - 1, 8, ACT), F32),
            pltpu.VMEM((8, ACT), F32),
            pltpu.VMEM((ZS - 1, 8, ACT), F32),
        ]

    return (
        [
            pltpu.VMEM((13, STARS), F32),
            pltpu.VMEM((1, STARS), F32),
            pltpu.VMEM((1, ACT), jnp.int32),
            pltpu.VMEM((ROWS, 8, STARS), F32),
        ]
        + sums()
        + [
            pltpu.VMEM((ROWS * STARS, 128), BF16),
            pltpu.VMEM((CHUNKS, 32, 2 * CHUNK), BF16),
            pltpu.VMEM((ROWS, SPAN, ACT), BF16),
            pltpu.VMEM((128, 2 * ACT), BF16),
            pltpu.VMEM((128, 128), F32),
            pltpu.VMEM((32, ACT), F32),
            pltpu.VMEM((CHUNK, 2 * ACT), F32),
            pltpu.VMEM((CHUNK, 2 * ACT), F32),
            pltpu.VMEM((2 * CHUNK, ACT), BF16),
            pltpu.VMEM((2 * CHUNK, ACT), BF16),
        ]
        + sums()
        + [pltpu.VMEM((ROWS, 8, ACT), F32), dma((3,))]
        + [dma((n,)) for n in (YS - 1, YS - 1, YS, YS)]
        + [dma((n,)) for n in (XS - 1, XS - 1, ZS - 1, ZS - 1) * 2]
        + [dma((n,)) for n in (YS - 1, YS - 1, YS, YS)]
    )


def local(stars, elapsed, active_ids):
    return pl.pallas_call(
        kernel,
        out_shape=pltpu.VMEM((13, STARS), F32),
        in_specs=[HBM] * 3,
        out_specs=VMEM,
        scratch_shapes=scratch(),
        compiler_params=pltpu.CompilerParams(
            collective_id=0, has_side_effects=True, vmem_limit_bytes=56 << 20
        ),
        name="hermite_step",
    )(stars, elapsed.reshape(1, STARS), active_ids.reshape(1, ACT))


def solution(mesh):
    in_specs = (P(None, ("row", "col")), P(("row", "col")), P("row"))
    out_specs = P(None, ("row", "col"))
    return jax.shard_map(local, mesh=mesh, in_specs=in_specs, out_specs=out_specs, check_vma=False)
```

```python
import jax
import jax.numpy as jnp
import numpy as np
from jax import lax
from jax.experimental import pallas as pl
from jax.experimental.pallas import tpu as pltpu
from jax.sharding import PartitionSpec as P

SOFTEN = 0.0025
F32 = jnp.float32
BF16 = jnp.bfloat16
ROWS = 8
YS = 4
XS = 4
ZS = 8
COLS = XS * ZS
STARS = 2048
ACT = 512
CHUNK = 256
PER_SLOT = STARS // CHUNK
CHUNKS = ROWS * PER_SLOT
UNROLL = 16
HALF = 256
BLOCK = 64
SPAN = 256
GROUPS = STARS // SPAN
SPLIT_PAIRS = ((0, 0), (0, 1), (1, 0), (1, 1), (0, 2), (2, 0))
SOFTEN_HI = float(np.float32(SOFTEN).astype(jnp.bfloat16))
SOFTEN_LO = float(np.float32(SOFTEN - SOFTEN_HI).astype(jnp.bfloat16))
VMEM = pl.BlockSpec(memory_space=pltpu.VMEM)
HBM = pl.BlockSpec(memory_space=pl.ANY)


def split3(x):
    hi = x.astype(BF16).astype(F32)
    rest = x - hi
    mid = rest.astype(BF16).astype(F32)
    return hi, mid, rest - mid


def split_grid(x):
    coarse = jnp.floor(x * 8.0 + 0.5) * 0.125
    return coarse, x - coarse


def dot3(a, b):
    return jnp.sum(a * b, axis=0, keepdims=True)


def place():
    row = lax.axis_index("row")
    col = lax.axis_index("col")
    return row, col, row // 2, row % 2, col // ZS, col % ZS


def row_from(o):
    _, _, y, core, _, _ = place()
    return lax.rem(y + YS - o, YS) * 2 + core


def y_peer(o):
    _, col, y, core, _, _ = place()
    return (lax.rem(y + o, YS) * 2 + core, col)


def sibling():
    _, col, y, core, _, _ = place()
    return (y * 2 + 1 - core, col)


def x_peer(o):
    row, _, _, _, x, z = place()
    return (row, lax.rem(x + o, XS) * ZS + z)


def z_peer(o):
    row, _, _, _, x, z = place()
    return (row, x * ZS + lax.rem(z + o, ZS))


def send(src, dst, send_sem, recv_sem, peer):
    copy = pltpu.make_async_remote_copy(
        src_ref=src,
        dst_ref=dst,
        send_sem=send_sem,
        recv_sem=recv_sem,
        device_id=peer,
        device_id_type=pl.DeviceIdType.MESH,
    )
    copy.start()
    return copy


def dither(lanes):
    return 1.0 + ((lanes * 40503) & 127).astype(F32) * (1.0 / 128.0)


def field_rows(x, v):
    coarse, fine = split_grid(x)
    one = jnp.ones_like(x[0:1])
    zero = jnp.zeros_like(one)
    big = split3(dot3(coarse, coarse))
    small = split3(dot3(2.0 * coarse + fine, fine))
    hi, mid, lo = split3(fine)
    radial = split3(jnp.concatenate([v, x, dot3(x, v), one], 0))
    return jnp.concatenate(
        [*big, one, one, one, -2.0 * coarse]
        + [zero] * 7
        + [-2.0 * coarse] * 3
        + [hi, mid, lo, -2.0 * hi, -2.0 * hi, -2.0 * mid, -2.0 * mid, *small]
        + [one] * 5
        + [zero] * 10
        + [radial[q] for _, q in SPLIT_PAIRS]
        + [zero] * 16,
        0,
    )


def active_rows(x, v):
    coarse, fine = split_grid(x)
    one = jnp.ones_like(x[0:1])
    zero = jnp.zeros_like(one)
    big = split3(dot3(coarse, coarse))
    small = split3(dot3(2.0 * coarse + fine, fine))
    hi, mid, lo = split3(fine)
    radial = split3(jnp.concatenate([-x, -v, one, dot3(x, v)], 0))
    for_q = jnp.concatenate(
        [one, one, one, *big, coarse]
        + [zero] * 7
        + [hi, mid, lo]
        + [-2.0 * coarse] * 3
        + [hi, mid, hi, mid, one, one, one, *small, SOFTEN_HI * one, SOFTEN_LO * one]
        + [zero] * 74,
        0,
    )
    for_d = jnp.concatenate(
        [zero] * 64 + [radial[p] for p, _ in SPLIT_PAIRS] + [zero] * 16, 0
    )
    return jnp.concatenate([for_q, for_d], 1).astype(BF16)


def kernel(
    stars_in,
    elapsed_in,
    ids_in,
    out,
    stars,
    elapsed,
    ids,
    field,
    found,
    act_x,
    act_mid,
    act_z,
    feats,
    mix,
    spots,
    act_w,
    factor,
    accum,
    qd0,
    qd1,
    w0,
    w1,
    part,
    sum_x,
    sum_mid,
    sum_z,
    tot,
    in_sem,
    fy_s,
    fy_r,
    fc_s,
    fc_r,
    ax_s,
    ax_r,
    az_s,
    az_r,
    sx_s,
    sx_r,
    sz_s,
    sz_r,
    ty_s,
    ty_r,
    tc_s,
    tc_r,
):
    row, col, _, core, _, _ = place()
    loads = [
        pltpu.make_async_copy(src, dst, in_sem.at[i])
        for i, (src, dst) in enumerate(((stars_in, stars), (elapsed_in, elapsed), (ids_in, ids)))
    ]
    for c in loads:
        c.start()
    barrier = pltpu.get_barrier_semaphore()
    peers = (
        [sibling()]
        + [y_peer(o) for o in range(1, YS)]
        + [x_peer(o) for o in range(1, XS)]
        + [z_peer(o) for o in range(1, ZS)]
    )
    for peer in peers:
        pl.semaphore_signal(barrier, inc=1, device_id=peer, device_id_type=pl.DeviceIdType.MESH)
    for c in loads:
        c.wait()

    t = elapsed[...]
    x, v, a, j = stars[0:3, :], stars[3:6, :], stars[6:9, :], stars[9:12, :]
    x = x + t * (v + t * (a / 2.0 + t * j / 6.0))
    v = v + t * (a + t * j / 2.0)
    field[row, 0:3, :] = x
    field[row, 3:6, :] = v
    field[row, 6:7, :] = stars[12:13, :]
    star = ids[...]
    field[row, 7:8, :] = jnp.concatenate([star.astype(F32), jnp.zeros((1, STARS - ACT), F32)], 1)
    centre_x = jnp.floor(jnp.sum(x, axis=1, keepdims=True) * (8.0 / STARS) + 0.5) * 0.125
    centre_v = jnp.floor(jnp.sum(v, axis=1, keepdims=True) * (8.0 / STARS) + 0.5) * 0.125
    pl.semaphore_wait(barrier, len(peers))

    waits = []
    own = field.at[row]
    over_y = {o: send(own, own, fy_s.at[o - 1], fy_r.at[o - 1], y_peer(o)) for o in (1, 3, 2)}
    over_core = [send(own, own, fc_s.at[0], fc_r.at[0], sibling())]

    owner = star // STARS
    code = jnp.where(owner % COLS == col, owner // COLS * 16 + star % STARS // 128, -1)
    one_hot = jnp.where(
        lax.broadcasted_iota(jnp.int32, (128, ACT), 0) == star % 128, 1.0, 0.0
    ).astype(BF16)
    one_hot = jnp.concatenate([one_hot] * 3, 0)

    def pick(r):
        block = jnp.concatenate([field[r, :, g * 128 : (g + 1) * 128] for g in range(16)], 0)
        parts = jnp.concatenate(split3(block), 1).astype(BF16)
        hits = jnp.dot(parts, one_hot, preferred_element_type=F32)
        total = jnp.zeros((8, ACT), F32)
        for g in range(16):
            total = total + jnp.where(code == r * 16 + g, hits[g * 8 : (g + 1) * 8], 0.0)
        found[...] += total

    found[...] = jnp.zeros_like(found)
    pick(row)
    for o in (1, 3, 2):
        over_y[o].wait_recv()
        block = field.at[row_from(o)]
        over_core.append(send(block, block, fc_s.at[o], fc_r.at[o], sibling()))
        pick(row_from(o))
    for c, o in zip(over_core, (0, 1, 3, 2)):
        c.wait_recv()
        pick(row_from(o) + 1 - 2 * core)
    waits += list(over_y.values()) + over_core

    lanes = lax.broadcasted_iota(jnp.int32, (1, STARS), 1)
    lane_of = lax.broadcasted_iota(jnp.int32, (SPAN, ACT), 0)

    def operands(r, _):
        f = field[r]
        x, v, mass = f[0:3] - centre_x, f[3:6] - centre_v, f[6:7]
        rows = field_rows(x, v)
        for b in range(STARS // 128):
            at = pl.ds(pl.multiple_of(r * STARS + b * 128, 128), 128)
            feats[at, :] = jnp.transpose(rows[:, b * 128 : (b + 1) * 128]).astype(BF16)
        m = mass / dither(lanes & 127)
        zero = jnp.zeros_like(m)
        by_w = jnp.concatenate([m * x, m * v, m, zero], 0)
        m = -3.0 * m
        by_v = jnp.concatenate([zero, zero, zero, m * x, zero, m], 0)
        pad = jnp.zeros((8, STARS), F32)
        by_w = jnp.concatenate([*split3(by_w), pad], 0).astype(BF16)
        by_v = jnp.concatenate([*split3(by_v), pad], 0).astype(BF16)
        for c in range(PER_SLOT):
            cut = slice(c * CHUNK, (c + 1) * CHUNK)
            mix[r * PER_SLOT + c] = jnp.concatenate([by_w[:, cut], by_v[:, cut]], 1)
        at = f[7:8, 0:ACT].astype(jnp.int32) % SPAN
        spots[r] = jnp.where(lane_of == at, 1.0, 0.0).astype(BF16)
        return 0

    copies = [
        send(found, act_x.at[o - 1], ax_s.at[o - 1], ax_r.at[o - 1], x_peer(o))
        for o in range(1, XS)
    ]
    factor[...] = dither(lax.broadcasted_iota(jnp.int32, (128, 128), 0))
    lax.fori_loop(0, 4, operands, 0)
    for c in copies:
        c.wait_recv()
    waits += copies
    act_mid[...] = (found[...] + act_x[0]) + (act_x[1] + act_x[2])
    copies = [
        send(act_mid, act_z.at[o - 1], az_s.at[o - 1], az_r.at[o - 1], z_peer(o))
        for o in range(1, ZS)
    ]
    lax.fori_loop(4, ROWS, operands, 0)
    accum[...] = jnp.zeros_like(accum)
    w1[...] = jnp.zeros_like(w1)
    for c in copies:
        c.wait_recv()
    waits += copies
    act = act_mid[...]
    for o in range(ZS - 1):
        act = act + act_z[o]
    xa, va = act[0:3] - centre_x, act[3:6] - centre_v
    act_w[...] = active_rows(xa, va)

    def products(c, qd, h, z):
        at = pl.ds(pl.multiple_of(c * CHUNK, CHUNK), CHUNK)
        cut = slice(z * ACT + h * HALF, z * ACT + (h + 1) * HALF)
        qd[:, cut] = jnp.dot(feats[at, :], act_w[:, cut], preferred_element_type=F32)

    def sums(c, w, h):
        cut = slice(h * HALF, (h + 1) * HALF)
        accum[:, cut] += jnp.dot(mix[c], w[:, cut], preferred_element_type=F32)

    def step(c, qd, w_now, w_before):
        before = jnp.maximum(c - 1, 0)
        for h in range(ACT // HALF):
            products(c, qd, h, 0)
            products(c, qd, h, 1)
            sums(before, w_before, h)
        for b in range(CHUNK // BLOCK):
            down = slice(b * BLOCK, (b + 1) * BLOCK)
            below = slice(CHUNK + b * BLOCK, CHUNK + (b + 1) * BLOCK)
            f = factor[b * BLOCK % 128 : b * BLOCK % 128 + BLOCK, :]
            for h in range(ACT // 128):
                cut = slice(h * 128, (h + 1) * 128)
                inv = lax.rsqrt(qd[down, cut])
                inv2 = inv * inv
                w = (inv * f) * inv2
                w_now[down, cut] = w.astype(BF16)
                d = qd[down, ACT + h * 128 : ACT + (h + 1) * 128]
                w_now[below, cut] = (w * (inv2 * d)).astype(BF16)

    def steps(i, _):
        for u in range(0, UNROLL, 2):
            step(UNROLL * i + u, qd0, w0, w1)
            step(UNROLL * i + u + 1, qd1, w1, w0)
        return 0

    lax.fori_loop(0, CHUNKS // UNROLL, steps, 0)
    for h in range(ACT // HALF):
        sums(CHUNKS - 1, w1, h)
    o = accum[...]
    o = o[0:8] + o[8:16] + o[16:24]
    part[0:3, :] = o[0:3] - xa * o[6:7]
    part[3:6, :] = o[3:6] - va * o[6:7] - xa * o[7:8]
    part[6:8, :] = jnp.zeros((2, ACT), F32)

    copies = [
        send(part, sum_x.at[o - 1], sx_s.at[o - 1], sx_r.at[o - 1], x_peer(o))
        for o in range(1, XS)
    ]
    for c in copies:
        c.wait_recv()
    waits += copies
    sum_mid[...] = (part[...] + sum_x[0]) + (sum_x[1] + sum_x[2])
    copies = [
        send(sum_mid, sum_z.at[o - 1], sz_s.at[o - 1], sz_r.at[o - 1], z_peer(o))
        for o in range(1, ZS)
    ]
    for c in copies:
        c.wait_recv()
    waits += copies
    total = ((sum_mid[...] + sum_z[0]) + (sum_z[1] + sum_z[2])) + (
        (sum_z[3] + sum_z[4]) + (sum_z[5] + sum_z[6])
    )
    tot[row, 0:6, :] = total[0:6]
    tot[row, 6:7, :] = jnp.zeros((1, ACT), F32)
    tot[row, 7:8, :] = jnp.ones((1, ACT), F32)
    own = tot.at[row]
    over_y = {o: send(own, own, ty_s.at[o - 1], ty_r.at[o - 1], y_peer(o)) for o in (1, 3, 2)}
    over_core = [send(own, own, tc_s.at[0], tc_r.at[0], sibling())]

    first = (row * COLS + col) * STARS

    def scatter(r):
        local = field[r, 7:8, 0:ACT].astype(jnp.int32) - first
        group = jnp.where((local >= 0) & (local < STARS), local // SPAN, -1)
        parts = jnp.concatenate(split3(tot[r]), 0)
        lhs = jnp.concatenate([jnp.where(group == g, parts, 0.0) for g in range(GROUPS)], 0)
        return lax.dot_general(
            lhs.astype(BF16), spots[r], (((1,), (1,)), ((), ())), preferred_element_type=F32
        )

    placed = scatter(row)
    for o in (1, 3, 2):
        over_y[o].wait_recv()
        block = tot.at[row_from(o)]
        over_core.append(send(block, block, tc_s.at[o], tc_r.at[o], sibling()))
        placed = placed + scatter(row_from(o))
    for c, o in zip(over_core, (0, 1, 3, 2)):
        c.wait_recv()
        placed = placed + scatter(row_from(o) + 1 - 2 * core)
    waits += list(over_y.values()) + over_core
    new = jnp.concatenate(
        [
            placed[g * 24 : g * 24 + 8]
            + placed[g * 24 + 8 : g * 24 + 16]
            + placed[g * 24 + 16 : g * 24 + 24]
            for g in range(GROUPS)
        ],
        1,
    )
    acc_new, jerk_new, hit = new[0:3], new[3:6], new[7:8] > 0.5
    t = elapsed[...]
    x, v, a, j = stars[0:3, :], stars[3:6, :], stars[6:9, :], stars[9:12, :]
    v1 = v + (a + acc_new) * t / 2.0 + (j - jerk_new) * t * t / 12.0
    x1 = x + (v + v1) * t / 2.0 + (a - acc_new) * t * t / 12.0
    out[0:3, :] = jnp.where(hit, x1, x)
    out[3:6, :] = jnp.where(hit, v1, v)
    out[6:9, :] = jnp.where(hit, acc_new, a)
    out[9:12, :] = jnp.where(hit, jerk_new, j)
    out[12:13, :] = stars[12:13, :]
    for c in waits:
        c.wait_send()


def scratch():
    dma = pltpu.SemaphoreType.DMA

    def sums():
        return [
            pltpu.VMEM((8, ACT), F32),
            pltpu.VMEM((XS - 1, 8, ACT), F32),
            pltpu.VMEM((8, ACT), F32),
            pltpu.VMEM((ZS - 1, 8, ACT), F32),
        ]

    return (
        [
            pltpu.VMEM((13, STARS), F32),
            pltpu.VMEM((1, STARS), F32),
            pltpu.VMEM((1, ACT), jnp.int32),
            pltpu.VMEM((ROWS, 8, STARS), F32),
        ]
        + sums()
        + [
            pltpu.VMEM((ROWS * STARS, 128), BF16),
            pltpu.VMEM((CHUNKS, 32, 2 * CHUNK), BF16),
            pltpu.VMEM((ROWS, SPAN, ACT), BF16),
            pltpu.VMEM((128, 2 * ACT), BF16),
            pltpu.VMEM((128, 128), F32),
            pltpu.VMEM((32, ACT), F32),
            pltpu.VMEM((CHUNK, 2 * ACT), F32),
            pltpu.VMEM((CHUNK, 2 * ACT), F32),
            pltpu.VMEM((2 * CHUNK, ACT), BF16),
            pltpu.VMEM((2 * CHUNK, ACT), BF16),
        ]
        + sums()
        + [pltpu.VMEM((ROWS, 8, ACT), F32), dma((3,))]
        + [dma((n,)) for n in (YS - 1, YS - 1, YS, YS)]
        + [dma((n,)) for n in (XS - 1, XS - 1, ZS - 1, ZS - 1) * 2]
        + [dma((n,)) for n in (YS - 1, YS - 1, YS, YS)]
    )


def local(stars, elapsed, active_ids):
    return pl.pallas_call(
        kernel,
        out_shape=pltpu.VMEM((13, STARS), F32),
        in_specs=[HBM] * 3,
        out_specs=VMEM,
        scratch_shapes=scratch(),
        compiler_params=pltpu.CompilerParams(
            collective_id=0, has_side_effects=True, vmem_limit_bytes=56 << 20
        ),
        name="hermite_step",
    )(stars, elapsed.reshape(1, STARS), active_ids.reshape(1, ACT))


def solution(mesh):
    in_specs = (P(None, ("row", "col")), P(("row", "col")), P("row"))
    out_specs = P(None, ("row", "col"))
    return jax.shard_map(local, mesh=mesh, in_specs=in_specs, out_specs=out_specs, check_vma=False)
```

```python
import jax
import jax.numpy as jnp
import numpy as np
from jax import lax
from jax.experimental import pallas as pl
from jax.experimental.pallas import tpu as pltpu
from jax.sharding import PartitionSpec as P

SOFTEN = 0.0025
F32 = jnp.float32
BF16 = jnp.bfloat16
ROWS = 8
YS = 4
XS = 4
ZS = 8
COLS = XS * ZS
STARS = 2048
ACT = 512
CHUNK = 256
PER_SLOT = STARS // CHUNK
CHUNKS = ROWS * PER_SLOT
UNROLL = 16
HALF = 256
BLOCK = 64
Y_ORDER = (2, 1, 3)
X_ORDER = (2, 1, 3)
Z_ORDER = (4, 3, 5, 2, 6, 1, 7)
PLANE = [(oy, ox) for oy in (2, 1, 3, 0) for ox in (2, 1, 3, 0) if (oy, ox) != (0, 0)]
SPAN = 256
GROUPS = STARS // SPAN
SPLIT_PAIRS = ((0, 0), (0, 1), (1, 0), (1, 1), (0, 2), (2, 0))
SOFTEN_HI = float(np.float32(SOFTEN).astype(jnp.bfloat16))
SOFTEN_LO = float(np.float32(SOFTEN - SOFTEN_HI).astype(jnp.bfloat16))
VMEM = pl.BlockSpec(memory_space=pltpu.VMEM)
HBM = pl.BlockSpec(memory_space=pl.ANY)


def split3(x):
    hi = x.astype(BF16).astype(F32)
    rest = x - hi
    mid = rest.astype(BF16).astype(F32)
    return hi, mid, rest - mid


def split_grid(x):
    coarse = jnp.floor(x * 8.0 + 0.5) * 0.125
    return coarse, x - coarse


def dot3(a, b):
    return jnp.sum(a * b, axis=0, keepdims=True)


def place():
    row = lax.axis_index("row")
    col = lax.axis_index("col")
    return row, col, row // 2, row % 2, col // ZS, col % ZS


def row_from(o):
    _, _, y, core, _, _ = place()
    return lax.rem(y + YS - o, YS) * 2 + core


def sibling():
    _, col, y, core, _, _ = place()
    return (y * 2 + 1 - core, col)


def cross_peer(o):
    _, _, y, core, x, z = place()
    return (y * 2 + 1 - core, lax.rem(x + o, XS) * ZS + z)


def plane_peer(oy, ox):
    _, _, y, core, x, z = place()
    return (lax.rem(y + oy, YS) * 2 + core, lax.rem(x + ox, XS) * ZS + z)


def z_peer(o):
    row, _, _, _, x, z = place()
    return (row, x * ZS + lax.rem(z + o, ZS))


def send(src, dst, send_sem, recv_sem, peer):
    copy = pltpu.make_async_remote_copy(
        src_ref=src,
        dst_ref=dst,
        send_sem=send_sem,
        recv_sem=recv_sem,
        device_id=peer,
        device_id_type=pl.DeviceIdType.MESH,
    )
    copy.start()
    return copy


def pack(values):
    return jnp.concatenate([values[0:6, t * 128 : (t + 1) * 128] for t in range(ACT // 128)], 0)


def unpack(tiles):
    return jnp.concatenate([tiles[6 * t : 6 * t + 6] for t in range(ACT // 128)], 1)


def dither(lanes):
    return 1.0 + ((lanes * 40503) & 127).astype(F32) * (1.0 / 128.0)


def field_rows(x, v):
    coarse, fine = split_grid(x)
    one = jnp.ones_like(x[0:1])
    zero = jnp.zeros_like(one)
    big = split3(dot3(coarse, coarse))
    small = split3(dot3(2.0 * coarse + fine, fine))
    hi, mid, lo = split3(fine)
    radial = split3(jnp.concatenate([v, x, dot3(x, v), one], 0))
    return jnp.concatenate(
        [*big, one, one, one, -2.0 * coarse]
        + [zero] * 7
        + [-2.0 * coarse] * 3
        + [hi, mid, lo, -2.0 * hi, -2.0 * hi, -2.0 * mid, -2.0 * mid, *small]
        + [one] * 5
        + [zero] * 10
        + [radial[q] for _, q in SPLIT_PAIRS]
        + [zero] * 16,
        0,
    )


def active_rows(x, v):
    coarse, fine = split_grid(x)
    one = jnp.ones_like(x[0:1])
    zero = jnp.zeros_like(one)
    big = split3(dot3(coarse, coarse))
    small = split3(dot3(2.0 * coarse + fine, fine))
    hi, mid, lo = split3(fine)
    radial = split3(jnp.concatenate([-x, -v, one, dot3(x, v)], 0))
    for_q = jnp.concatenate(
        [one, one, one, *big, coarse]
        + [zero] * 7
        + [hi, mid, lo]
        + [-2.0 * coarse] * 3
        + [hi, mid, hi, mid, one, one, one, *small, SOFTEN_HI * one, SOFTEN_LO * one]
        + [zero] * 74,
        0,
    )
    for_d = jnp.concatenate(
        [zero] * 64 + [radial[p] for p, _ in SPLIT_PAIRS] + [zero] * 16, 0
    )
    return jnp.concatenate([for_q, for_d], 1).astype(BF16)


def kernel(
    stars_in,
    elapsed_in,
    ids_in,
    out,
    stars,
    elapsed,
    ids,
    field,
    found,
    act_x,
    act_mid,
    act_z,
    feats,
    mix,
    spots,
    act_w,
    factor,
    accum,
    qd0,
    qd1,
    w0,
    w1,
    part,
    sum_z,
    plane,
    tot,
    in_sem,
    fy_s,
    fy_r,
    fc_s,
    fc_r,
    ax_s,
    ax_r,
    az_s,
    az_r,
    sz_s,
    sz_r,
    sp_s,
    sp_r,
    tc_s,
    tc_r,
):
    row, col, y_at, core, x_at, _ = place()
    other = row + 1 - 2 * core
    loads = [
        pltpu.make_async_copy(src, dst, in_sem.at[i])
        for i, (src, dst) in enumerate(((stars_in, stars), (elapsed_in, elapsed), (ids_in, ids)))
    ]
    for c in loads:
        c.start()
    barrier = pltpu.get_barrier_semaphore()
    peers = (
        [sibling()]
        + [plane_peer(oy, ox) for oy, ox in PLANE]
        + [cross_peer(o) for o in range(1, XS)]
        + [z_peer(o) for o in range(1, ZS)]
    )
    for peer in peers:
        pl.semaphore_signal(barrier, inc=1, device_id=peer, device_id_type=pl.DeviceIdType.MESH)
    for c in loads:
        c.wait()

    t = elapsed[...]
    x, v, a, j = stars[0:3, :], stars[3:6, :], stars[6:9, :], stars[9:12, :]
    x = x + t * (v + t * (a / 2.0 + t * j / 6.0))
    v = v + t * (a + t * j / 2.0)
    field[row, 0:3, :] = x
    field[row, 3:6, :] = v
    field[row, 6:7, :] = stars[12:13, :]
    star = ids[...]
    field[row, 7:8, :] = jnp.concatenate([star.astype(F32), jnp.zeros((1, STARS - ACT), F32)], 1)
    pl.semaphore_wait(barrier, len(peers))

    waits = []
    own = field.at[row]
    over_y = {o: send(own, own, fy_s.at[o - 1], fy_r.at[o - 1], plane_peer(o, 0)) for o in Y_ORDER}
    over_core = [send(own, own, fc_s.at[0], fc_r.at[0], sibling())]
    centre_x = jnp.floor(jnp.sum(x, axis=1, keepdims=True) * (8.0 / STARS) + 0.5) * 0.125
    centre_v = jnp.floor(jnp.sum(v, axis=1, keepdims=True) * (8.0 / STARS) + 0.5) * 0.125

    over_core[0].wait_recv()
    star = jnp.concatenate([star, field[other, 7:8, 0:ACT].astype(jnp.int32)], 1)
    owner = star // STARS
    code = jnp.where(owner % COLS == col, owner // COLS * 16 + star % STARS // 128, -1)
    one_hot = jnp.where(
        lax.broadcasted_iota(jnp.int32, (128, 2 * ACT), 0) == star % 128, 1.0, 0.0
    ).astype(BF16)
    one_hot = jnp.concatenate([one_hot] * 3, 0)

    def pick(r, total):
        block = jnp.concatenate([field[r, :, g * 128 : (g + 1) * 128] for g in range(16)], 0)
        parts = jnp.concatenate(split3(block), 1).astype(BF16)
        hits = jnp.dot(parts, one_hot, preferred_element_type=F32)
        for g in range(16):
            total = total + jnp.where(code == r * 16 + g, hits[g * 8 : (g + 1) * 8], 0.0)
        return total

    picks = pick(row, jnp.zeros((8, 2 * ACT), F32))
    for o in (1, 3, 2):
        over_y[o].wait_recv()
        block = field.at[row_from(o)]
        over_core.append(send(block, block, fc_s.at[o], fc_r.at[o], sibling()))
        picks = pick(row_from(o), picks)
    found[0] = pack(picks[:, 0:ACT])
    found[1] = pack(picks[:, ACT : 2 * ACT])
    waits += list(over_y.values()) + over_core

    lanes = lax.broadcasted_iota(jnp.int32, (1, STARS), 1)
    lane_of = lax.broadcasted_iota(jnp.int32, (SPAN, ACT), 0)

    def operands(r, _):
        f = field[r]
        x, v, mass = f[0:3] - centre_x, f[3:6] - centre_v, f[6:7]
        rows = field_rows(x, v)
        for b in range(STARS // 128):
            at = pl.ds(pl.multiple_of(r * STARS + b * 128, 128), 128)
            feats[at, :] = jnp.transpose(rows[:, b * 128 : (b + 1) * 128]).astype(BF16)
        m = mass / dither(lanes & 127)
        zero = jnp.zeros_like(m)
        by_w = jnp.concatenate([m * x, m * v, m, zero], 0)
        m = -3.0 * m
        by_v = jnp.concatenate([zero, zero, zero, m * x, zero, m], 0)
        pad = jnp.zeros((8, STARS), F32)
        by_w = jnp.concatenate([*split3(by_w), pad], 0).astype(BF16)
        by_v = jnp.concatenate([*split3(by_v), pad], 0).astype(BF16)
        for c in range(PER_SLOT):
            cut = slice(c * CHUNK, (c + 1) * CHUNK)
            mix[r * PER_SLOT + c] = jnp.concatenate([by_w[:, cut], by_v[:, cut]], 1)
        at = f[7:8, 0:ACT].astype(jnp.int32) % SPAN
        spots[r] = jnp.where(lane_of == at, 1.0, 0.0).astype(BF16)
        return 0

    copies = []
    for o in X_ORDER + (0,):
        copies.append(send(found.at[1], act_x.at[o], ax_s.at[o], ax_r.at[o], cross_peer(o)))
        if o:
            n = XS + o - 1
            copies.append(
                send(found.at[0], act_x.at[n], ax_s.at[n], ax_r.at[n], plane_peer(0, o))
            )
    for c in over_core[1:]:
        c.wait_recv()
    factor[...] = dither(lax.broadcasted_iota(jnp.int32, (128, 128), 0))
    lax.fori_loop(0, 4, operands, 0)
    for c in copies:
        c.wait_recv()
    waits += copies
    mine = found[0]
    for o in range(2 * XS - 1):
        mine = mine + act_x[o]
    act_mid[...] = mine
    copies = [
        send(act_mid, act_z.at[o - 1], az_s.at[o - 1], az_r.at[o - 1], z_peer(o))
        for o in Z_ORDER
    ]
    lax.fori_loop(4, ROWS, operands, 0)
    accum[...] = jnp.zeros_like(accum)
    w1[...] = jnp.zeros_like(w1)
    for c in copies:
        c.wait_recv()
    waits += copies
    for o in range(ZS - 1):
        mine = mine + act_z[o]
    act = unpack(mine)
    xa, va = act[0:3] - centre_x, act[3:6] - centre_v
    act_w[...] = active_rows(xa, va)

    def products(c, qd, h, z):
        at = pl.ds(pl.multiple_of(c * CHUNK, CHUNK), CHUNK)
        cut = slice(z * ACT + h * HALF, z * ACT + (h + 1) * HALF)
        qd[:, cut] = jnp.dot(feats[at, :], act_w[:, cut], preferred_element_type=F32)

    def sums(c, w, h):
        cut = slice(h * HALF, (h + 1) * HALF)
        accum[:, cut] += jnp.dot(mix[c], w[:, cut], preferred_element_type=F32)

    def step(c, qd, w_now, w_before):
        before = jnp.maximum(c - 1, 0)
        for h in range(ACT // HALF):
            products(c, qd, h, 0)
            products(c, qd, h, 1)
            sums(before, w_before, h)
        for b in range(CHUNK // BLOCK):
            down = slice(b * BLOCK, (b + 1) * BLOCK)
            below = slice(CHUNK + b * BLOCK, CHUNK + (b + 1) * BLOCK)
            f = factor[b * BLOCK % 128 : b * BLOCK % 128 + BLOCK, :]
            for h in range(ACT // 128):
                cut = slice(h * 128, (h + 1) * 128)
                inv = lax.rsqrt(qd[down, cut])
                inv2 = inv * inv
                w = (inv * f) * inv2
                w_now[down, cut] = w.astype(BF16)
                d = qd[down, ACT + h * 128 : ACT + (h + 1) * 128]
                w_now[below, cut] = (w * (inv2 * d)).astype(BF16)

    def steps(i, _):
        for u in range(0, UNROLL, 2):
            step(UNROLL * i + u, qd0, w0, w1)
            step(UNROLL * i + u + 1, qd1, w1, w0)
        return 0

    lax.fori_loop(0, CHUNKS // UNROLL, steps, 0)
    for h in range(ACT // HALF):
        sums(CHUNKS - 1, w1, h)
    o = accum[...]
    o = o[0:8] + o[8:16] + o[16:24]
    part[...] = pack(
        jnp.concatenate([o[0:3] - xa * o[6:7], o[3:6] - va * o[6:7] - xa * o[7:8]], 0)
    )

    copies = [
        send(part, sum_z.at[o - 1], sz_s.at[o - 1], sz_r.at[o - 1], z_peer(o)) for o in Z_ORDER
    ]
    for c in copies:
        c.wait_recv()
    waits += copies
    plane[y_at, x_at] = ((part[...] + sum_z[0]) + (sum_z[1] + sum_z[2])) + (
        (sum_z[3] + sum_z[4]) + (sum_z[5] + sum_z[6])
    )
    own = plane.at[y_at, x_at]
    over_plane = {}
    for oy, ox in PLANE:
        n = oy * XS + ox
        over_plane[oy, ox] = send(own, own, sp_s.at[n], sp_r.at[n], plane_peer(oy, ox))

    first = (row * COLS + col) * STARS

    def scatter(r):
        local = field[r, 7:8, 0:ACT].astype(jnp.int32) - first
        group = jnp.where((local >= 0) & (local < STARS), local // SPAN, -1)
        ones = jnp.ones((1, ACT), F32)
        rows = jnp.concatenate([unpack(tot[r]), 0.0 * ones, ones], 0)
        parts = jnp.concatenate(split3(rows), 0)
        lhs = jnp.concatenate([jnp.where(group == g, parts, 0.0) for g in range(GROUPS)], 0)
        return lax.dot_general(
            lhs.astype(BF16), spots[r], (((1,), (1,)), ((), ())), preferred_element_type=F32
        )

    placed = jnp.zeros((GROUPS * 24, SPAN), F32)
    over_core = []
    for oy in (0, 1, 3, 2):
        for ox in (1, 3, 2, 0):
            if (oy, ox) in over_plane:
                over_plane[oy, ox].wait_recv()
        y = lax.rem(y_at + YS - oy, YS)
        r = row_from(oy)
        tot[r] = (plane[y, 0] + plane[y, 1]) + (plane[y, 2] + plane[y, 3])
        block = tot.at[r]
        over_core.append(send(block, block, tc_s.at[oy], tc_r.at[oy], sibling()))
        placed = placed + scatter(r)
    for c, oy in zip(over_core, (0, 1, 3, 2)):
        c.wait_recv()
        placed = placed + scatter(row_from(oy) + 1 - 2 * core)
    waits += list(over_plane.values()) + over_core
    new = jnp.concatenate(
        [
            placed[g * 24 : g * 24 + 8]
            + placed[g * 24 + 8 : g * 24 + 16]
            + placed[g * 24 + 16 : g * 24 + 24]
            for g in range(GROUPS)
        ],
        1,
    )
    acc_new, jerk_new, hit = new[0:3], new[3:6], new[7:8] > 0.5
    t = elapsed[...]
    x, v, a, j = stars[0:3, :], stars[3:6, :], stars[6:9, :], stars[9:12, :]
    v1 = v + (a + acc_new) * t / 2.0 + (j - jerk_new) * t * t / 12.0
    x1 = x + (v + v1) * t / 2.0 + (a - acc_new) * t * t / 12.0
    out[0:3, :] = jnp.where(hit, x1, x)
    out[3:6, :] = jnp.where(hit, v1, v)
    out[6:9, :] = jnp.where(hit, acc_new, a)
    out[9:12, :] = jnp.where(hit, jerk_new, j)
    out[12:13, :] = stars[12:13, :]
    for c in waits:
        c.wait_send()


def scratch():
    dma = pltpu.SemaphoreType.DMA
    packed = (6 * ACT // 128, 128)
    return (
        [
            pltpu.VMEM((13, STARS), F32),
            pltpu.VMEM((1, STARS), F32),
            pltpu.VMEM((1, ACT), jnp.int32),
            pltpu.VMEM((ROWS, 8, STARS), F32),
            pltpu.VMEM((2, *packed), F32),
            pltpu.VMEM((2 * XS - 1, *packed), F32),
            pltpu.VMEM(packed, F32),
            pltpu.VMEM((ZS - 1, *packed), F32),
            pltpu.VMEM((ROWS * STARS, 128), BF16),
            pltpu.VMEM((CHUNKS, 32, 2 * CHUNK), BF16),
            pltpu.VMEM((ROWS, SPAN, ACT), BF16),
            pltpu.VMEM((128, 2 * ACT), BF16),
            pltpu.VMEM((128, 128), F32),
            pltpu.VMEM((32, ACT), F32),
            pltpu.VMEM((CHUNK, 2 * ACT), F32),
            pltpu.VMEM((CHUNK, 2 * ACT), F32),
            pltpu.VMEM((2 * CHUNK, ACT), BF16),
            pltpu.VMEM((2 * CHUNK, ACT), BF16),
            pltpu.VMEM(packed, F32),
            pltpu.VMEM((ZS - 1, *packed), F32),
            pltpu.VMEM((YS, XS, *packed), F32),
            pltpu.VMEM((ROWS, *packed), F32),
            dma((3,)),
        ]
        + [dma((n,)) for n in (YS - 1, YS - 1, YS, YS)]
        + [dma((n,)) for n in (2 * XS - 1, 2 * XS - 1)]
        + [dma((n,)) for n in (ZS - 1, ZS - 1) * 2]
        + [dma((n,)) for n in (YS * XS, YS * XS, YS, YS)]
    )


def local(stars, elapsed, active_ids):
    return pl.pallas_call(
        kernel,
        out_shape=pltpu.VMEM((13, STARS), F32),
        in_specs=[HBM] * 3,
        out_specs=VMEM,
        scratch_shapes=scratch(),
        compiler_params=pltpu.CompilerParams(
            collective_id=0, has_side_effects=True, vmem_limit_bytes=56 << 20
        ),
        name="hermite_step",
    )(stars, elapsed.reshape(1, STARS), active_ids.reshape(1, ACT))


def solution(mesh):
    in_specs = (P(None, ("row", "col")), P(("row", "col")), P("row"))
    out_specs = P(None, ("row", "col"))
    return jax.shard_map(local, mesh=mesh, in_specs=in_specs, out_specs=out_specs, check_vma=False)
```

```python
import jax
import jax.numpy as jnp
import numpy as np
from jax import lax
from jax.experimental import pallas as pl
from jax.experimental.pallas import tpu as pltpu
from jax.sharding import PartitionSpec as P

SOFTEN = 0.0025
F32 = jnp.float32
BF16 = jnp.bfloat16
ROWS = 8
YS = 4
XS = 4
ZS = 8
COLS = XS * ZS
STARS = 2048
ACT = 512
CHUNK = 256
PER_SLOT = STARS // CHUNK
CHUNKS = ROWS * PER_SLOT
UNROLL = 16
HALF = 256
BLOCK = 64
Y_ORDER = (2, 1, 3)
X_ORDER = (2, 1, 3)
Z_ORDER = (4, 3, 5, 2, 6, 1, 7)
PLANE = [(oy, ox) for oy in (2, 1, 3, 0) for ox in (2, 1, 3, 0) if (oy, ox) != (0, 0)]
SPAN = 256
GROUPS = STARS // SPAN
SOFTEN_HI = float(np.float32(SOFTEN).astype(jnp.bfloat16))
SOFTEN_LO = float(np.float32(SOFTEN - SOFTEN_HI).astype(jnp.bfloat16))
VMEM = pl.BlockSpec(memory_space=pltpu.VMEM)
HBM = pl.BlockSpec(memory_space=pl.ANY)


def split3(x):
    hi = x.astype(BF16).astype(F32)
    rest = x - hi
    mid = rest.astype(BF16).astype(F32)
    return hi, mid, rest - mid


def split_grid(x):
    coarse = jnp.floor(x * 8.0 + 0.5) * 0.125
    return coarse, x - coarse


def dot3(a, b):
    return jnp.sum(a * b, axis=0, keepdims=True)


def place():
    row = lax.axis_index("row")
    col = lax.axis_index("col")
    return row, col, row // 2, row % 2, col // ZS, col % ZS


def row_from(o):
    _, _, y, core, _, _ = place()
    return lax.rem(y + YS - o, YS) * 2 + core


def sibling():
    _, col, y, core, _, _ = place()
    return (y * 2 + 1 - core, col)


def cross_peer(o):
    _, _, y, core, x, z = place()
    return (y * 2 + 1 - core, lax.rem(x + o, XS) * ZS + z)


def plane_peer(oy, ox):
    _, _, y, core, x, z = place()
    return (lax.rem(y + oy, YS) * 2 + core, lax.rem(x + ox, XS) * ZS + z)


def z_peer(o):
    row, _, _, _, x, z = place()
    return (row, x * ZS + lax.rem(z + o, ZS))


def send(src, dst, send_sem, recv_sem, peer):
    copy = pltpu.make_async_remote_copy(
        src_ref=src,
        dst_ref=dst,
        send_sem=send_sem,
        recv_sem=recv_sem,
        device_id=peer,
        device_id_type=pl.DeviceIdType.MESH,
    )
    copy.start()
    return copy


def pack(values):
    return jnp.concatenate([values[0:6, t * 128 : (t + 1) * 128] for t in range(ACT // 128)], 0)


def unpack(tiles):
    return jnp.concatenate([tiles[6 * t : 6 * t + 6] for t in range(ACT // 128)], 1)


def dither(lanes):
    return 1.0 + ((lanes * 40503) & 127).astype(F32) * (1.0 / 128.0)


def field_rows(x, v):
    coarse, fine = split_grid(x)
    coarse_v, fine_v = split_grid(v)
    one = jnp.ones_like(x[0:1])
    zero = jnp.zeros_like(one)
    big = split3(dot3(coarse, coarse))
    small = split3(dot3(2.0 * coarse + fine, fine))
    big_d = split3(dot3(coarse, coarse_v))
    small_d = split3(dot3(coarse, fine_v) + dot3(fine, v))
    hi, mid, lo = split3(fine)
    hi_v, mid_v, lo_v = split3(fine_v)
    return jnp.concatenate(
        [*big, one, one, one, -2.0 * coarse, *big_d, coarse_v, zero]
        + [-2.0 * coarse] * 3
        + [hi, mid, lo, -2.0 * hi, -2.0 * hi, -2.0 * mid, -2.0 * mid, *small]
        + [one] * 5
        + [*small_d, hi_v, mid_v, lo_v, coarse_v, coarse_v, coarse_v, hi_v, hi_v, mid_v, mid_v]
        + [zero] * 41,
        0,
    )


def active_rows(x, v):
    coarse, fine = split_grid(x)
    coarse_v, fine_v = split_grid(v)
    one = jnp.ones_like(x[0:1])
    zero = jnp.zeros_like(one)
    big = split3(dot3(coarse, coarse))
    small = split3(dot3(2.0 * coarse + fine, fine))
    big_d = split3(dot3(coarse, coarse_v))
    small_d = split3(dot3(coarse, fine_v) + dot3(fine, v))
    hi, mid, lo = split3(fine)
    hi_v, mid_v, lo_v = split3(0.5 * fine_v)
    for_q = jnp.concatenate(
        [one, one, one, *big, coarse]
        + [zero] * 7
        + [hi, mid, lo]
        + [-2.0 * coarse] * 3
        + [hi, mid, hi, mid, one, one, one, *small, SOFTEN_HI * one, SOFTEN_LO * one]
        + [zero] * 74,
        0,
    )
    for_d = jnp.concatenate(
        [zero, zero, zero, *big_d, 0.5 * coarse_v, one, one, one, -coarse, zero]
        + [hi_v, mid_v, lo_v]
        + [-coarse_v] * 3
        + [hi_v, mid_v, hi_v, mid_v, zero, zero, zero, *small_d, zero, zero, one, one, one]
        + [-coarse] * 3
        + [-hi, -mid, -lo, -hi, -mid, -hi, -mid]
        + [zero] * 41,
        0,
    )
    return jnp.concatenate([for_q, for_d], 1).astype(BF16)


def kernel(
    stars_in,
    elapsed_in,
    ids_in,
    out,
    stars,
    elapsed,
    ids,
    field,
    found,
    act_x,
    act_mid,
    act_z,
    feats,
    mix,
    spots,
    act_w,
    factor,
    accum,
    qd0,
    qd1,
    w0,
    w1,
    part,
    sum_z,
    plane,
    tot,
    in_sem,
    fy_s,
    fy_r,
    fc_s,
    fc_r,
    ax_s,
    ax_r,
    az_s,
    az_r,
    sz_s,
    sz_r,
    sp_s,
    sp_r,
    tc_s,
    tc_r,
):
    row, col, y_at, core, x_at, _ = place()
    other = row + 1 - 2 * core
    loads = [
        pltpu.make_async_copy(src, dst, in_sem.at[i])
        for i, (src, dst) in enumerate(((stars_in, stars), (elapsed_in, elapsed), (ids_in, ids)))
    ]
    for c in loads:
        c.start()
    barrier = pltpu.get_barrier_semaphore()
    peers = (
        [sibling()]
        + [plane_peer(oy, ox) for oy, ox in PLANE]
        + [cross_peer(o) for o in range(1, XS)]
        + [z_peer(o) for o in range(1, ZS)]
    )
    for peer in peers:
        pl.semaphore_signal(barrier, inc=1, device_id=peer, device_id_type=pl.DeviceIdType.MESH)
    for c in loads:
        c.wait()

    t = elapsed[...]
    x, v, a, j = stars[0:3, :], stars[3:6, :], stars[6:9, :], stars[9:12, :]
    x = x + t * (v + t * (a / 2.0 + t * j / 6.0))
    v = v + t * (a + t * j / 2.0)
    field[row, 0:3, :] = x
    field[row, 3:6, :] = v
    field[row, 6:7, :] = stars[12:13, :]
    star = ids[...]
    field[row, 7:8, :] = jnp.concatenate([star.astype(F32), jnp.zeros((1, STARS - ACT), F32)], 1)
    pl.semaphore_wait(barrier, len(peers))

    waits = []
    own = field.at[row]
    over_y = {o: send(own, own, fy_s.at[o - 1], fy_r.at[o - 1], plane_peer(o, 0)) for o in Y_ORDER}
    over_core = [send(own, own, fc_s.at[0], fc_r.at[0], sibling())]
    centre_x = jnp.floor(jnp.sum(x, axis=1, keepdims=True) * (8.0 / STARS) + 0.5) * 0.125
    centre_v = jnp.floor(jnp.sum(v, axis=1, keepdims=True) * (8.0 / STARS) + 0.5) * 0.125

    over_core[0].wait_recv()
    star = jnp.concatenate([star, field[other, 7:8, 0:ACT].astype(jnp.int32)], 1)
    owner = star // STARS
    code = jnp.where(owner % COLS == col, owner // COLS * 16 + star % STARS // 128, -1)
    one_hot = jnp.where(
        lax.broadcasted_iota(jnp.int32, (128, 2 * ACT), 0) == star % 128, 1.0, 0.0
    ).astype(BF16)
    one_hot = jnp.concatenate([one_hot] * 3, 0)

    def pick(r, total):
        block = jnp.concatenate([field[r, :, g * 128 : (g + 1) * 128] for g in range(16)], 0)
        parts = jnp.concatenate(split3(block), 1).astype(BF16)
        hits = jnp.dot(parts, one_hot, preferred_element_type=F32)
        for g in range(16):
            total = total + jnp.where(code == r * 16 + g, hits[g * 8 : (g + 1) * 8], 0.0)
        return total

    picks = pick(row, jnp.zeros((8, 2 * ACT), F32))
    for o in (1, 3, 2):
        over_y[o].wait_recv()
        block = field.at[row_from(o)]
        over_core.append(send(block, block, fc_s.at[o], fc_r.at[o], sibling()))
        picks = pick(row_from(o), picks)
    found[0] = pack(picks[:, 0:ACT])
    found[1] = pack(picks[:, ACT : 2 * ACT])
    waits += list(over_y.values()) + over_core

    lanes = lax.broadcasted_iota(jnp.int32, (1, STARS), 1)
    lane_of = lax.broadcasted_iota(jnp.int32, (SPAN, ACT), 0)

    def operands(r, _):
        f = field[r]
        x, v, mass = f[0:3] - centre_x, f[3:6] - centre_v, f[6:7]
        rows = field_rows(x, v)
        for b in range(STARS // 128):
            at = pl.ds(pl.multiple_of(r * STARS + b * 128, 128), 128)
            feats[at, :] = jnp.transpose(rows[:, b * 128 : (b + 1) * 128]).astype(BF16)
        m = mass / dither(lanes & 127)
        zero = jnp.zeros_like(m)
        by_w = jnp.concatenate([m * x, m * v, m, zero], 0)
        m = -3.0 * m
        by_v = jnp.concatenate([zero, zero, zero, m * x, zero, m], 0)
        pad = jnp.zeros((8, STARS), F32)
        by_w = jnp.concatenate([*split3(by_w), pad], 0).astype(BF16)
        by_v = jnp.concatenate([*split3(by_v), pad], 0).astype(BF16)
        for c in range(PER_SLOT):
            cut = slice(c * CHUNK, (c + 1) * CHUNK)
            mix[r * PER_SLOT + c] = jnp.concatenate([by_w[:, cut], by_v[:, cut]], 1)
        at = f[7:8, 0:ACT].astype(jnp.int32) % SPAN
        spots[r] = jnp.where(lane_of == at, 1.0, 0.0).astype(BF16)
        return 0

    copies = []
    for o in X_ORDER + (0,):
        copies.append(send(found.at[1], act_x.at[o], ax_s.at[o], ax_r.at[o], cross_peer(o)))
        if o:
            n = XS + o - 1
            copies.append(
                send(found.at[0], act_x.at[n], ax_s.at[n], ax_r.at[n], plane_peer(0, o))
            )
    for c in over_core[1:]:
        c.wait_recv()
    factor[...] = dither(lax.broadcasted_iota(jnp.int32, (128, 128), 0))
    lax.fori_loop(0, 4, operands, 0)
    for c in copies:
        c.wait_recv()
    waits += copies
    mine = found[0]
    for o in range(2 * XS - 1):
        mine = mine + act_x[o]
    act_mid[...] = mine
    copies = [
        send(act_mid, act_z.at[o - 1], az_s.at[o - 1], az_r.at[o - 1], z_peer(o))
        for o in Z_ORDER
    ]
    lax.fori_loop(4, ROWS, operands, 0)
    accum[...] = jnp.zeros_like(accum)
    w1[...] = jnp.zeros_like(w1)
    for c in copies:
        c.wait_recv()
    waits += copies
    for o in range(ZS - 1):
        mine = mine + act_z[o]
    act = unpack(mine)
    xa, va = act[0:3] - centre_x, act[3:6] - centre_v
    act_w[...] = active_rows(xa, va)

    def products(c, qd, h, z):
        at = pl.ds(pl.multiple_of(c * CHUNK, CHUNK), CHUNK)
        cut = slice(z * ACT + h * HALF, z * ACT + (h + 1) * HALF)
        qd[:, cut] = jnp.dot(feats[at, :], act_w[:, cut], preferred_element_type=F32)

    def sums(c, w, h):
        cut = slice(h * HALF, (h + 1) * HALF)
        accum[:, cut] += jnp.dot(mix[c], w[:, cut], preferred_element_type=F32)

    def step(c, qd, w_now, w_before):
        before = jnp.maximum(c - 1, 0)
        for h in range(ACT // HALF):
            products(c, qd, h, 0)
            products(c, qd, h, 1)
            sums(before, w_before, h)
        for b in range(CHUNK // BLOCK):
            down = slice(b * BLOCK, (b + 1) * BLOCK)
            below = slice(CHUNK + b * BLOCK, CHUNK + (b + 1) * BLOCK)
            f = factor[b * BLOCK % 128 : b * BLOCK % 128 + BLOCK, :]
            for h in range(ACT // 128):
                cut = slice(h * 128, (h + 1) * 128)
                inv = lax.rsqrt(qd[down, cut])
                inv2 = inv * inv
                w = (inv * f) * inv2
                w_now[down, cut] = w.astype(BF16)
                d = qd[down, ACT + h * 128 : ACT + (h + 1) * 128]
                w_now[below, cut] = (w * (inv2 * d)).astype(BF16)

    def steps(i, _):
        for u in range(0, UNROLL, 2):
            step(UNROLL * i + u, qd0, w0, w1)
            step(UNROLL * i + u + 1, qd1, w1, w0)
        return 0

    lax.fori_loop(0, CHUNKS // UNROLL, steps, 0)
    for h in range(ACT // HALF):
        sums(CHUNKS - 1, w1, h)
    o = accum[...]
    o = o[0:8] + o[8:16] + o[16:24]
    part[...] = pack(
        jnp.concatenate([o[0:3] - xa * o[6:7], o[3:6] - va * o[6:7] - xa * o[7:8]], 0)
    )

    copies = [
        send(part, sum_z.at[o - 1], sz_s.at[o - 1], sz_r.at[o - 1], z_peer(o)) for o in Z_ORDER
    ]
    for c in copies:
        c.wait_recv()
    waits += copies
    plane[y_at, x_at] = ((part[...] + sum_z[0]) + (sum_z[1] + sum_z[2])) + (
        (sum_z[3] + sum_z[4]) + (sum_z[5] + sum_z[6])
    )
    own = plane.at[y_at, x_at]
    over_plane = {}
    for oy, ox in PLANE:
        n = oy * XS + ox
        over_plane[oy, ox] = send(own, own, sp_s.at[n], sp_r.at[n], plane_peer(oy, ox))

    first = (row * COLS + col) * STARS

    def scatter(r):
        local = field[r, 7:8, 0:ACT].astype(jnp.int32) - first
        group = jnp.where((local >= 0) & (local < STARS), local // SPAN, -1)
        ones = jnp.ones((1, ACT), F32)
        rows = jnp.concatenate([unpack(tot[r]), 0.0 * ones, ones], 0)
        parts = jnp.concatenate(split3(rows), 0)
        lhs = jnp.concatenate([jnp.where(group == g, parts, 0.0) for g in range(GROUPS)], 0)
        return lax.dot_general(
            lhs.astype(BF16), spots[r], (((1,), (1,)), ((), ())), preferred_element_type=F32
        )

    placed = jnp.zeros((GROUPS * 24, SPAN), F32)
    over_core = []
    for oy in (0, 1, 3, 2):
        for ox in (1, 3, 2, 0):
            if (oy, ox) in over_plane:
                over_plane[oy, ox].wait_recv()
        y = lax.rem(y_at + YS - oy, YS)
        r = row_from(oy)
        tot[r] = (plane[y, 0] + plane[y, 1]) + (plane[y, 2] + plane[y, 3])
        block = tot.at[r]
        over_core.append(send(block, block, tc_s.at[oy], tc_r.at[oy], sibling()))
        placed = placed + scatter(r)
    for c, oy in zip(over_core, (0, 1, 3, 2)):
        c.wait_recv()
        placed = placed + scatter(row_from(oy) + 1 - 2 * core)
    waits += list(over_plane.values()) + over_core
    new = jnp.concatenate(
        [
            placed[g * 24 : g * 24 + 8]
            + placed[g * 24 + 8 : g * 24 + 16]
            + placed[g * 24 + 16 : g * 24 + 24]
            for g in range(GROUPS)
        ],
        1,
    )
    acc_new, jerk_new, hit = new[0:3], new[3:6], new[7:8] > 0.5
    t = elapsed[...]
    x, v, a, j = stars[0:3, :], stars[3:6, :], stars[6:9, :], stars[9:12, :]
    v1 = v + (a + acc_new) * t / 2.0 + (j - jerk_new) * t * t / 12.0
    x1 = x + (v + v1) * t / 2.0 + (a - acc_new) * t * t / 12.0
    out[0:3, :] = jnp.where(hit, x1, x)
    out[3:6, :] = jnp.where(hit, v1, v)
    out[6:9, :] = jnp.where(hit, acc_new, a)
    out[9:12, :] = jnp.where(hit, jerk_new, j)
    out[12:13, :] = stars[12:13, :]
    for c in waits:
        c.wait_send()


def scratch():
    dma = pltpu.SemaphoreType.DMA
    packed = (6 * ACT // 128, 128)
    return (
        [
            pltpu.VMEM((13, STARS), F32),
            pltpu.VMEM((1, STARS), F32),
            pltpu.VMEM((1, ACT), jnp.int32),
            pltpu.VMEM((ROWS, 8, STARS), F32),
            pltpu.VMEM((2, *packed), F32),
            pltpu.VMEM((2 * XS - 1, *packed), F32),
            pltpu.VMEM(packed, F32),
            pltpu.VMEM((ZS - 1, *packed), F32),
            pltpu.VMEM((ROWS * STARS, 128), BF16),
            pltpu.VMEM((CHUNKS, 32, 2 * CHUNK), BF16),
            pltpu.VMEM((ROWS, SPAN, ACT), BF16),
            pltpu.VMEM((128, 2 * ACT), BF16),
            pltpu.VMEM((128, 128), F32),
            pltpu.VMEM((32, ACT), F32),
            pltpu.VMEM((CHUNK, 2 * ACT), F32),
            pltpu.VMEM((CHUNK, 2 * ACT), F32),
            pltpu.VMEM((2 * CHUNK, ACT), BF16),
            pltpu.VMEM((2 * CHUNK, ACT), BF16),
            pltpu.VMEM(packed, F32),
            pltpu.VMEM((ZS - 1, *packed), F32),
            pltpu.VMEM((YS, XS, *packed), F32),
            pltpu.VMEM((ROWS, *packed), F32),
            dma((3,)),
        ]
        + [dma((n,)) for n in (YS - 1, YS - 1, YS, YS)]
        + [dma((n,)) for n in (2 * XS - 1, 2 * XS - 1)]
        + [dma((n,)) for n in (ZS - 1, ZS - 1) * 2]
        + [dma((n,)) for n in (YS * XS, YS * XS, YS, YS)]
    )


def local(stars, elapsed, active_ids):
    return pl.pallas_call(
        kernel,
        out_shape=pltpu.VMEM((13, STARS), F32),
        in_specs=[HBM] * 3,
        out_specs=VMEM,
        scratch_shapes=scratch(),
        compiler_params=pltpu.CompilerParams(
            collective_id=0, has_side_effects=True, vmem_limit_bytes=56 << 20
        ),
        name="hermite_step",
    )(stars, elapsed.reshape(1, STARS), active_ids.reshape(1, ACT))


def solution(mesh):
    in_specs = (P(None, ("row", "col")), P(("row", "col")), P("row"))
    out_specs = P(None, ("row", "col"))
    return jax.shard_map(local, mesh=mesh, in_specs=in_specs, out_specs=out_specs, check_vma=False)
```

```python
import jax
import jax.numpy as jnp
import numpy as np
from jax import lax
from jax.experimental import pallas as pl
from jax.experimental.pallas import tpu as pltpu
from jax.sharding import PartitionSpec as P

SOFTEN = 0.0025
F32 = jnp.float32
BF16 = jnp.bfloat16
ROWS = 8
YS = 4
XS = 4
ZS = 8
COLS = XS * ZS
STARS = 2048
ACT = 512
CHUNK = 256
PER_SLOT = STARS // CHUNK
CHUNKS = ROWS * PER_SLOT
UNROLL = 32
HALF = 256
BLOCK = 64
Y_ORDER = (2, 1, 3)
X_ORDER = (2, 1, 3)
Z_ORDER = (4, 3, 5, 2, 6, 1, 7)
PLANE = [(2, 2), (2, 1), (2, 3), (1, 2), (3, 2), (1, 1), (1, 3), (3, 1), (3, 3)]
PLANE += [(2, 0), (0, 2), (1, 0), (3, 0), (0, 1), (0, 3)]
SPAN = 256
GROUPS = STARS // SPAN
SOFTEN_HI = float(np.float32(SOFTEN).astype(jnp.bfloat16))
SOFTEN_LO = float(np.float32(SOFTEN - SOFTEN_HI).astype(jnp.bfloat16))
VMEM = pl.BlockSpec(memory_space=pltpu.VMEM)
HBM = pl.BlockSpec(memory_space=pl.ANY)


def split3(x):
    hi = x.astype(BF16).astype(F32)
    rest = x - hi
    mid = rest.astype(BF16).astype(F32)
    return hi, mid, rest - mid


def split_grid(x):
    coarse = jnp.floor(x * 8.0 + 0.5) * 0.125
    return coarse, x - coarse


def dot3(a, b):
    return jnp.sum(a * b, axis=0, keepdims=True)


def place():
    row = lax.axis_index("row")
    col = lax.axis_index("col")
    return row, col, row // 2, row % 2, col // ZS, col % ZS


def row_from(o):
    _, _, y, core, _, _ = place()
    return lax.rem(y + YS - o, YS) * 2 + core


def sibling():
    _, col, y, core, _, _ = place()
    return (y * 2 + 1 - core, col)


def cross_peer(o):
    _, _, y, core, x, z = place()
    return (y * 2 + 1 - core, lax.rem(x + o, XS) * ZS + z)


def plane_peer(oy, ox):
    _, _, y, core, x, z = place()
    return (lax.rem(y + oy, YS) * 2 + core, lax.rem(x + ox, XS) * ZS + z)


def z_peer(o):
    row, _, _, _, x, z = place()
    return (row, x * ZS + lax.rem(z + o, ZS))


def send(src, dst, send_sem, recv_sem, peer):
    copy = pltpu.make_async_remote_copy(
        src_ref=src,
        dst_ref=dst,
        send_sem=send_sem,
        recv_sem=recv_sem,
        device_id=peer,
        device_id_type=pl.DeviceIdType.MESH,
    )
    copy.start()
    return copy


def pack(values):
    return jnp.concatenate([values[0:6, t * 128 : (t + 1) * 128] for t in range(ACT // 128)], 0)


def unpack(tiles):
    return jnp.concatenate([tiles[6 * t : 6 * t + 6] for t in range(ACT // 128)], 1)


def dither(lanes):
    return 1.0 + ((lanes * 40503) & 127).astype(F32) * (1.0 / 128.0)


def field_rows(x, v):
    coarse, fine = split_grid(x)
    coarse_v, fine_v = split_grid(v)
    one = jnp.ones_like(x[0:1])
    zero = jnp.zeros_like(one)
    big = split3(dot3(coarse, coarse))
    small = split3(dot3(2.0 * coarse + fine, fine))
    big_d = split3(dot3(coarse, coarse_v))
    small_d = split3(dot3(coarse, fine_v) + dot3(fine, v))
    hi, mid, lo = split3(fine)
    hi_v, mid_v, lo_v = split3(fine_v)
    return jnp.concatenate(
        [*big, one, one, one, -2.0 * coarse, *big_d, coarse_v, zero]
        + [-2.0 * coarse] * 3
        + [hi, mid, lo, -2.0 * hi, -2.0 * hi, -2.0 * mid, -2.0 * mid, *small]
        + [one] * 5
        + [*small_d, hi_v, mid_v, lo_v, coarse_v, coarse_v, coarse_v, hi_v, hi_v, mid_v, mid_v]
        + [zero] * 41,
        0,
    )


def active_rows(x, v):
    coarse, fine = split_grid(x)
    coarse_v, fine_v = split_grid(v)
    one = jnp.ones_like(x[0:1])
    zero = jnp.zeros_like(one)
    big = split3(dot3(coarse, coarse))
    small = split3(dot3(2.0 * coarse + fine, fine))
    big_d = split3(dot3(coarse, coarse_v))
    small_d = split3(dot3(coarse, fine_v) + dot3(fine, v))
    hi, mid, lo = split3(fine)
    hi_v, mid_v, lo_v = split3(0.5 * fine_v)
    for_q = jnp.concatenate(
        [one, one, one, *big, coarse]
        + [zero] * 7
        + [hi, mid, lo]
        + [-2.0 * coarse] * 3
        + [hi, mid, hi, mid, one, one, one, *small, SOFTEN_HI * one, SOFTEN_LO * one]
        + [zero] * 74,
        0,
    )
    for_d = jnp.concatenate(
        [zero, zero, zero, *big_d, 0.5 * coarse_v, one, one, one, -coarse, zero]
        + [hi_v, mid_v, lo_v]
        + [-coarse_v] * 3
        + [hi_v, mid_v, hi_v, mid_v, zero, zero, zero, *small_d, zero, zero, one, one, one]
        + [-coarse] * 3
        + [-hi, -mid, -lo, -hi, -mid, -hi, -mid]
        + [zero] * 41,
        0,
    )
    return jnp.concatenate([for_q, for_d], 1).astype(BF16)


def kernel(
    stars_in,
    elapsed_in,
    ids_in,
    out,
    stars,
    elapsed,
    ids,
    field,
    found,
    act_x,
    act_mid,
    act_z,
    feats,
    mix,
    spots,
    act_w,
    factor,
    accum,
    qd0,
    qd1,
    w0,
    w1,
    part,
    sum_z,
    plane,
    tot,
    in_sem,
    fy_s,
    fy_r,
    fc_s,
    fc_r,
    ax_s,
    ax_r,
    az_s,
    az_r,
    sz_s,
    sz_r,
    sp_s,
    sp_r,
    tc_s,
    tc_r,
):
    row, col, y_at, core, x_at, _ = place()
    other = row + 1 - 2 * core
    loads = [
        pltpu.make_async_copy(src, dst, in_sem.at[i])
        for i, (src, dst) in enumerate(((stars_in, stars), (elapsed_in, elapsed), (ids_in, ids)))
    ]
    for c in loads:
        c.start()
    barrier = pltpu.get_barrier_semaphore()
    peers = (
        [z_peer(o) for o in Z_ORDER]
        + [plane_peer(oy, ox) for oy, ox in PLANE]
        + [cross_peer(o) for o in X_ORDER]
        + [sibling()]
    )
    for peer in peers:
        pl.semaphore_signal(barrier, inc=1, device_id=peer, device_id_type=pl.DeviceIdType.MESH)
    for c in loads:
        c.wait()

    t = elapsed[...]
    x, v, a, j = stars[0:3, :], stars[3:6, :], stars[6:9, :], stars[9:12, :]
    x = x + t * (v + t * (a / 2.0 + t * j / 6.0))
    v = v + t * (a + t * j / 2.0)
    field[row, 0:3, :] = x
    field[row, 3:6, :] = v
    field[row, 6:7, :] = stars[12:13, :]
    star = ids[...]
    field[row, 7:8, :] = jnp.concatenate([star.astype(F32), jnp.zeros((1, STARS - ACT), F32)], 1)
    pl.semaphore_wait(barrier, len(peers))

    waits = []
    own = field.at[row]
    over_y = {o: send(own, own, fy_s.at[o - 1], fy_r.at[o - 1], plane_peer(o, 0)) for o in Y_ORDER}
    over_core = [send(own, own, fc_s.at[0], fc_r.at[0], sibling())]
    centre_x = jnp.floor(jnp.sum(x, axis=1, keepdims=True) * (8.0 / STARS) + 0.5) * 0.125
    centre_v = jnp.floor(jnp.sum(v, axis=1, keepdims=True) * (8.0 / STARS) + 0.5) * 0.125

    over_core[0].wait_recv()
    star = jnp.concatenate([star, field[other, 7:8, 0:ACT].astype(jnp.int32)], 1)
    owner = star // STARS
    code = jnp.where(owner % COLS == col, owner // COLS * 16 + star % STARS // 128, -1)
    one_hot = jnp.where(
        lax.broadcasted_iota(jnp.int32, (128, 2 * ACT), 0) == star % 128, 1.0, 0.0
    ).astype(BF16)
    one_hot = jnp.concatenate([one_hot] * 3, 0)

    def pick(r, total):
        block = jnp.concatenate([field[r, :, g * 128 : (g + 1) * 128] for g in range(16)], 0)
        parts = jnp.concatenate(split3(block), 1).astype(BF16)
        hits = jnp.dot(parts, one_hot, preferred_element_type=F32)
        for g in range(16):
            total = total + jnp.where(code == r * 16 + g, hits[g * 8 : (g + 1) * 8], 0.0)
        return total

    picks = pick(row, jnp.zeros((8, 2 * ACT), F32))
    for o in (1, 3, 2):
        over_y[o].wait_recv()
        block = field.at[row_from(o)]
        over_core.append(send(block, block, fc_s.at[o], fc_r.at[o], sibling()))
        picks = pick(row_from(o), picks)
    found[0] = pack(picks[:, 0:ACT])
    found[1] = pack(picks[:, ACT : 2 * ACT])
    waits += list(over_y.values()) + over_core

    lanes = lax.broadcasted_iota(jnp.int32, (1, STARS), 1)
    lane_of = lax.broadcasted_iota(jnp.int32, (SPAN, ACT), 0)

    def operands(r, _):
        f = field[r]
        x, v, mass = f[0:3] - centre_x, f[3:6] - centre_v, f[6:7]
        rows = field_rows(x, v)
        for b in range(STARS // 128):
            at = pl.ds(pl.multiple_of(r * STARS + b * 128, 128), 128)
            feats[at, :] = jnp.transpose(rows[:, b * 128 : (b + 1) * 128]).astype(BF16)
        m = mass / dither(lanes & 127)
        zero = jnp.zeros_like(m)
        by_w = jnp.concatenate([m * x, m * v, m, zero], 0)
        m = -3.0 * m
        by_v = jnp.concatenate([zero, zero, zero, m * x, zero, m], 0)
        pad = jnp.zeros((8, STARS), F32)
        by_w = jnp.concatenate([*split3(by_w), pad], 0).astype(BF16)
        by_v = jnp.concatenate([*split3(by_v), pad], 0).astype(BF16)
        for c in range(PER_SLOT):
            cut = slice(c * CHUNK, (c + 1) * CHUNK)
            mix[r * PER_SLOT + c] = jnp.concatenate([by_w[:, cut], by_v[:, cut]], 1)
        at = f[7:8, 0:ACT].astype(jnp.int32) % SPAN
        spots[r] = jnp.where(lane_of == at, 1.0, 0.0).astype(BF16)
        return 0

    copies = []
    for o in X_ORDER + (0,):
        copies.append(send(found.at[1], act_x.at[o], ax_s.at[o], ax_r.at[o], cross_peer(o)))
        if o:
            n = XS + o - 1
            copies.append(
                send(found.at[0], act_x.at[n], ax_s.at[n], ax_r.at[n], plane_peer(0, o))
            )
    for c in over_core[1:]:
        c.wait_recv()
    factor[...] = dither(lax.broadcasted_iota(jnp.int32, (128, 128), 0))
    lax.fori_loop(0, 4, operands, 0)
    for c in copies:
        c.wait_recv()
    waits += copies
    mine = found[0]
    for o in range(2 * XS - 1):
        mine = mine + act_x[o]
    act_mid[...] = mine
    copies = [
        send(act_mid, act_z.at[o - 1], az_s.at[o - 1], az_r.at[o - 1], z_peer(o))
        for o in Z_ORDER
    ]
    lax.fori_loop(4, ROWS, operands, 0)
    accum[...] = jnp.zeros_like(accum)
    w1[...] = jnp.zeros_like(w1)
    for c in copies:
        c.wait_recv()
    waits += copies
    for o in range(ZS - 1):
        mine = mine + act_z[o]
    act = unpack(mine)
    xa, va = act[0:3] - centre_x, act[3:6] - centre_v
    act_w[...] = active_rows(xa, va)

    def products(c, qd, h, z):
        at = pl.ds(pl.multiple_of(c * CHUNK, CHUNK), CHUNK)
        cut = slice(z * ACT + h * HALF, z * ACT + (h + 1) * HALF)
        qd[:, cut] = jnp.dot(feats[at, :], act_w[:, cut], preferred_element_type=F32)

    def sums(c, w, h):
        cut = slice(h * HALF, (h + 1) * HALF)
        accum[:, cut] += jnp.dot(mix[c], w[:, cut], preferred_element_type=F32)

    def step(c, qd, w_now, w_before):
        before = jnp.maximum(c - 1, 0)
        for h in range(ACT // HALF):
            products(c, qd, h, 0)
            products(c, qd, h, 1)
            sums(before, w_before, h)
        for b in range(CHUNK // BLOCK):
            down = slice(b * BLOCK, (b + 1) * BLOCK)
            below = slice(CHUNK + b * BLOCK, CHUNK + (b + 1) * BLOCK)
            f = factor[b * BLOCK % 128 : b * BLOCK % 128 + BLOCK, :]
            for h in range(ACT // 128):
                cut = slice(h * 128, (h + 1) * 128)
                inv = lax.rsqrt(qd[down, cut])
                inv2 = inv * inv
                w = (inv * f) * inv2
                w_now[down, cut] = w.astype(BF16)
                d = qd[down, ACT + h * 128 : ACT + (h + 1) * 128]
                w_now[below, cut] = (w * (inv2 * d)).astype(BF16)

    def steps(i, _):
        for u in range(0, UNROLL, 2):
            step(UNROLL * i + u, qd0, w0, w1)
            step(UNROLL * i + u + 1, qd1, w1, w0)
        return 0

    lax.fori_loop(0, CHUNKS // UNROLL, steps, 0)
    for h in range(ACT // HALF):
        sums(CHUNKS - 1, w1, h)
    o = accum[...]
    o = o[0:8] + o[8:16] + o[16:24]
    part[...] = pack(
        jnp.concatenate([o[0:3] - xa * o[6:7], o[3:6] - va * o[6:7] - xa * o[7:8]], 0)
    )

    copies = [
        send(part, sum_z.at[o - 1], sz_s.at[o - 1], sz_r.at[o - 1], z_peer(o)) for o in Z_ORDER
    ]
    for c in copies:
        c.wait_recv()
    waits += copies
    plane[y_at, x_at] = ((part[...] + sum_z[0]) + (sum_z[1] + sum_z[2])) + (
        (sum_z[3] + sum_z[4]) + (sum_z[5] + sum_z[6])
    )
    own = plane.at[y_at, x_at]
    over_plane = {}
    for oy, ox in PLANE:
        n = oy * XS + ox
        over_plane[oy, ox] = send(own, own, sp_s.at[n], sp_r.at[n], plane_peer(oy, ox))

    first = (row * COLS + col) * STARS

    def scatter(r):
        local = field[r, 7:8, 0:ACT].astype(jnp.int32) - first
        group = jnp.where((local >= 0) & (local < STARS), local // SPAN, -1)
        ones = jnp.ones((1, ACT), F32)
        rows = jnp.concatenate([unpack(tot[r]), 0.0 * ones, ones], 0)
        parts = jnp.concatenate(split3(rows), 0)
        lhs = jnp.concatenate([jnp.where(group == g, parts, 0.0) for g in range(GROUPS)], 0)
        return lax.dot_general(
            lhs.astype(BF16), spots[r], (((1,), (1,)), ((), ())), preferred_element_type=F32
        )

    placed = jnp.zeros((GROUPS * 24, SPAN), F32)
    over_core = []
    for oy in (0, 1, 3, 2):
        for ox in (1, 3, 2, 0):
            if (oy, ox) in over_plane:
                over_plane[oy, ox].wait_recv()
        y = lax.rem(y_at + YS - oy, YS)
        r = row_from(oy)
        tot[r] = (plane[y, 0] + plane[y, 1]) + (plane[y, 2] + plane[y, 3])
        block = tot.at[r]
        over_core.append(send(block, block, tc_s.at[oy], tc_r.at[oy], sibling()))
        placed = placed + scatter(r)
    for c, oy in zip(over_core, (0, 1, 3, 2)):
        c.wait_recv()
        placed = placed + scatter(row_from(oy) + 1 - 2 * core)
    waits += list(over_plane.values()) + over_core
    new = jnp.concatenate(
        [
            placed[g * 24 : g * 24 + 8]
            + placed[g * 24 + 8 : g * 24 + 16]
            + placed[g * 24 + 16 : g * 24 + 24]
            for g in range(GROUPS)
        ],
        1,
    )
    acc_new, jerk_new, hit = new[0:3], new[3:6], new[7:8] > 0.5
    t = elapsed[...]
    x, v, a, j = stars[0:3, :], stars[3:6, :], stars[6:9, :], stars[9:12, :]
    v1 = v + (a + acc_new) * t / 2.0 + (j - jerk_new) * t * t / 12.0
    x1 = x + (v + v1) * t / 2.0 + (a - acc_new) * t * t / 12.0
    out[0:3, :] = jnp.where(hit, x1, x)
    out[3:6, :] = jnp.where(hit, v1, v)
    out[6:9, :] = jnp.where(hit, acc_new, a)
    out[9:12, :] = jnp.where(hit, jerk_new, j)
    out[12:13, :] = stars[12:13, :]
    for c in waits:
        c.wait_send()


def scratch():
    dma = pltpu.SemaphoreType.DMA
    packed = (6 * ACT // 128, 128)
    return (
        [
            pltpu.VMEM((13, STARS), F32),
            pltpu.VMEM((1, STARS), F32),
            pltpu.VMEM((1, ACT), jnp.int32),
            pltpu.VMEM((ROWS, 8, STARS), F32),
            pltpu.VMEM((2, *packed), F32),
            pltpu.VMEM((2 * XS - 1, *packed), F32),
            pltpu.VMEM(packed, F32),
            pltpu.VMEM((ZS - 1, *packed), F32),
            pltpu.VMEM((ROWS * STARS, 128), BF16),
            pltpu.VMEM((CHUNKS, 32, 2 * CHUNK), BF16),
            pltpu.VMEM((ROWS, SPAN, ACT), BF16),
            pltpu.VMEM((128, 2 * ACT), BF16),
            pltpu.VMEM((128, 128), F32),
            pltpu.VMEM((32, ACT), F32),
            pltpu.VMEM((CHUNK, 2 * ACT), F32),
            pltpu.VMEM((CHUNK, 2 * ACT), F32),
            pltpu.VMEM((2 * CHUNK, ACT), BF16),
            pltpu.VMEM((2 * CHUNK, ACT), BF16),
            pltpu.VMEM(packed, F32),
            pltpu.VMEM((ZS - 1, *packed), F32),
            pltpu.VMEM((YS, XS, *packed), F32),
            pltpu.VMEM((ROWS, *packed), F32),
            dma((3,)),
        ]
        + [dma((n,)) for n in (YS - 1, YS - 1, YS, YS)]
        + [dma((n,)) for n in (2 * XS - 1, 2 * XS - 1)]
        + [dma((n,)) for n in (ZS - 1, ZS - 1) * 2]
        + [dma((n,)) for n in (YS * XS, YS * XS, YS, YS)]
    )


def local(stars, elapsed, active_ids):
    return pl.pallas_call(
        kernel,
        out_shape=pltpu.VMEM((13, STARS), F32),
        in_specs=[HBM] * 3,
        out_specs=VMEM,
        scratch_shapes=scratch(),
        compiler_params=pltpu.CompilerParams(
            collective_id=0, has_side_effects=True, vmem_limit_bytes=56 << 20
        ),
        name="hermite_step",
    )(stars, elapsed.reshape(1, STARS), active_ids.reshape(1, ACT))


def solution(mesh):
    in_specs = (P(None, ("row", "col")), P(("row", "col")), P("row"))
    out_specs = P(None, ("row", "col"))
    return jax.shard_map(local, mesh=mesh, in_specs=in_specs, out_specs=out_specs, check_vma=False)
```
